256 devices in a mesh: head: 8 (over y, x_hi), tile: 32 (over z, x_lo, core).
Axes of the slice: x: 4 (x_hi: 2, x_lo: 2; x = x_hi * 2 + x_lo), y: 4, z: 8, core: 2. Of those that a mesh axis runs over, the one named last changes fastest.
Arguments:
- query: bfloat16 [32, 384, 2048], P('tile', None, 'head'), may hold values from -6 to 6
- key: bfloat16 [32, 384, 2048], P('tile', None, 'head'), may hold values from -6 to 6
- value: bfloat16 [32, 384, 2048], P('tile', None, 'head'), may hold values from -6 to 6
- grad_out: bfloat16 [32, 384, 2048], P('tile', 'head'), may hold values from -384 to 384
- gain_q: float32 [128], replicated, may hold values from 0.25 to 1.75
- gain_k: float32 [128], replicated, may hold values from 0.25 to 1.75
- window: int32 [16, 6], P('head'), may hold values from -1 to 1, as said below
Outputs:
- grad_query: bfloat16 [32, 384, 2048], P('tile', None, 'head')
- grad_key: bfloat16 [32, 384, 2048], P('tile', None, 'head')
- grad_value: bfloat16 [32, 384, 2048], P('tile', None, 'head')
The draws below stay inside these ranges and needn't reach their ends.
Inputs may be any that keep to these rules, and one draw needn't show every extreme that they name: `window`: columns 0, 2, 4 (lowest offsets along frames, rows, columns) are -1 or 0 and columns 1, 3, 5 (highest) are 0 or 1.
All inputs are finite; a program needn't handle non-finite values.
Results may differ from the reference program's by a relative error of at most 0.0092.
Values may be sent and summed in bfloat16 or wider, within the bound.
A program may use at most 128 MiB of HBM per device.

```python
import math
import jax
import jax.numpy as jnp
from jax import lax

HS = 128
HEADS = 16
TF = 4
TR = 2
TC = 4
TILES = 32
TILE_TOK = 384
HD = 2048


def draw_window(key, part):
    key = jax.random.fold_in(key, 7)
    reach = jax.random.randint(key, (HEADS, 6), 0, 4) > 0
    reach = reach.at[0].set(True)
    columns = []
    for index in (0, 2, 4):
        columns.append(-jnp.where(reach[:, index], 1, 0))
        columns.append(jnp.where(reach[:, index + 1], 1, 0))
    return jnp.stack(columns, axis=1).astype(jnp.int32)


def steps_of(rng, dims, split, smallest, top_value):
    def one(axis_at, shards_of):
        steps = jax.random.uniform(jax.random.fold_in(jax.random.fold_in(rng, 6), axis_at), (shards_of,), jnp.float32, smallest / len(split), top_value / len(split))
        return jnp.repeat(jnp.exp(steps), dims[axis_at] // shards_of).reshape((-1,) + (1,) * (len(dims) - axis_at - 1))

    level = one(*split[0])
    for cut in split[1:]:
        level = level * one(*cut)
    return level


def bell_draw(rng, shape, spread, bound, shards=(), kind=jnp.bfloat16):
    drawn = spread * jax.random.normal(rng, shape, jnp.float32)
    if shards:
        drawn = drawn * steps_of(rng, shape, shards, -0.22, 0.18)
    return jnp.clip(drawn, -bound, bound).astype(kind)


def setup_inputs(seed: int = 0) -> dict:
    keys = jax.random.split(jax.random.key(seed), 8)
    query = bell_draw(keys[0], (TILES, TILE_TOK, HD), 1.0, 6.0, ((0, 32), (2, 8)))
    key = bell_draw(keys[1], (TILES, TILE_TOK, HD), 1.0, 6.0, ((0, 32), (2, 8)))
    value = bell_draw(keys[2], (TILES, TILE_TOK, HD), 1.0, 6.0, ((0, 32), (2, 8)))
    grad_out = bell_draw(keys[3], (TILES, TILE_TOK, HD), 64.0, 384.0, ((0, 32), (1, 8)))
    gain_q = jnp.clip(1.0 + 0.15 * jax.random.normal(keys[4], (HS,), jnp.float32), 0.25, 1.75)
    gain_k = jnp.clip(1.0 + 0.15 * jax.random.normal(keys[5], (HS,), jnp.float32), 0.25, 1.75)
    window = draw_window(jax.random.fold_in(keys[7], 71), 0)
    return dict(query=query, key=key, value=value, grad_out=grad_out, gain_q=gain_q, gain_k=gain_k, window=window)


def normed(values_in, gain):
    floats = values_in.astype(jnp.float32)
    return floats * lax.rsqrt(lax.optimization_barrier(jnp.mean(floats * floats, axis=-1, keepdims=True)) + 1e-06) * gain

def norm_pullback(values_in, gain, cotangent):
    _, pull = jax.vjp(lambda inner: normed(inner, gain), values_in.astype(jnp.float32))
    return pull(cotangent)[0]

def reference(query, key, value, grad_out, gain_q, gain_k, window):
    query_heads = query.reshape(TILES, TILE_TOK, HEADS, HS)
    key_heads = key.reshape(TILES, TILE_TOK, HEADS, HS)
    value_heads = value.reshape(TILES, TILE_TOK, HEADS, HS).astype(jnp.float32)
    cotangent = grad_out.reshape(TILES, TILE_TOK, HEADS, HS).astype(jnp.float32)
    query_norm = normed(query_heads, gain_q).astype(jnp.bfloat16)
    key_norm = normed(key_heads, gain_k).astype(jnp.bfloat16)
    scale = 1.0 / math.sqrt(HS)
    tile_ids = jnp.arange(TILES, dtype=jnp.int32)
    offsets = jnp.arange(27, dtype=jnp.int32)
    off_frame = offsets // 9 - 1
    off_row = offsets // 3 % 3 - 1
    off_col = offsets % 3 - 1
    column = tile_ids % TC
    row_tile = tile_ids // TC % TR
    frame = tile_ids // (TC * TR)
    new_frame = frame[:, None] + off_frame[None, :]
    new_row = row_tile[:, None] + off_row[None, :]
    new_col = column[:, None] + off_col[None, :]
    inside = (new_frame >= 0) & (new_frame < TF) & (new_row >= 0) & (new_row < TR) & (new_col >= 0) & (new_col < TC)
    in_window = (off_frame[:, None] >= window[None, :, 0]) & (off_frame[:, None] <= window[None, :, 1])
    in_window = in_window & (off_row[:, None] >= window[None, :, 2]) & (off_row[:, None] <= window[None, :, 3])
    in_window = in_window & (off_col[:, None] >= window[None, :, 4]) & (off_col[:, None] <= window[None, :, 5])
    valid = inside[:, :, None] & in_window[None]
    neighbour = jnp.clip(tile_ids[:, None] + off_frame[None] * (TR * TC) + off_row[None] * TC + off_col[None], 0, TILES - 1).astype(jnp.int32)

    def one_tile(carry, tile_id):
        key_acc, value_acc = carry
        picked = neighbour[tile_id]
        allowed = jnp.repeat(valid[tile_id], TILE_TOK, axis=0).T
        keys_here = key_norm[picked].reshape(27 * TILE_TOK, HEADS, HS).astype(jnp.float32)
        values_here = value_heads[picked].reshape(27 * TILE_TOK, HEADS, HS)
        queries = query_norm[tile_id].astype(jnp.float32)
        cot_here = cotangent[tile_id]
        scores = jnp.einsum('qhd,khd->hqk', queries, keys_here) * scale
        unnorm = jnp.where(allowed[:, None, :], jnp.exp(scores), 0.0)
        totals = lax.optimization_barrier(jnp.sum(unnorm, axis=-1))
        probs = unnorm / totals[..., None]
        dprobs = jnp.einsum('qhd,khd->hqk', cot_here, values_here)
        centre = lax.optimization_barrier(jnp.sum(probs * dprobs, axis=-1))
        dscore = lax.optimization_barrier((probs * (dprobs - centre[..., None])).astype(jnp.bfloat16)).astype(jnp.float32)
        probs_low = lax.optimization_barrier(probs.astype(jnp.bfloat16)).astype(jnp.float32)
        dquery = jnp.einsum('hqk,khd->qhd', dscore, keys_here) * scale
        dkey = (jnp.einsum('hqk,qhd->khd', dscore, queries) * scale).reshape(27, TILE_TOK, HEADS, HS)
        dvalue = jnp.einsum('hqk,qhd->khd', probs_low, cot_here).reshape(27, TILE_TOK, HEADS, HS)
        key_acc = key_acc.at[picked].add(dkey)
        value_acc = value_acc.at[picked].add(dvalue)
        return ((key_acc, value_acc), dquery)
    empty = jnp.zeros((TILES, TILE_TOK, HEADS, HS), jnp.float32)
    (key_acc, value_acc), dquery_all = lax.scan(one_tile, (empty, empty), tile_ids)
    grad_query = norm_pullback(query_heads, gain_q, dquery_all).astype(jnp.bfloat16).reshape(TILES, TILE_TOK, HD)
    grad_key = norm_pullback(key_heads, gain_k, key_acc).astype(jnp.bfloat16).reshape(TILES, TILE_TOK, HD)
    grad_value = value_acc.astype(jnp.bfloat16).reshape(TILES, TILE_TOK, HD)
    return (grad_query, grad_key, grad_value)
```

```python
import math

import jax
import jax.numpy as jnp
from jax import lax
from jax.experimental import pallas as pl
from jax.experimental.pallas import tpu as pltpu
from jax.sharding import PartitionSpec as P

MESH = pl.DeviceIdType.MESH
HS = 128
TF, TR, TC = 4, 2, 4
ROWS = 384
PIECE = 48
GROUP = 8
PLANE = TR * TC
SCALE = 1.0 / math.sqrt(HS)
LOG2E = math.log2(math.e)
EXP_SCALE = SCALE * LOG2E
HIDE = 1e30
EPS = 1e-6

A2A = 0
KVROW = 8
KVCOL = 9
QF = 13
DOF = 15
PART = 17
TOTAL = 19
GCOL = 21
GROW = 25
GQ = 26
COPIES = 28


def dot(a, b):
    return jnp.dot(a, b, preferred_element_type=jnp.float32)


def fold8(x):
    return jnp.sum(x.reshape(x.shape[0] // 8, 8, x.shape[1]), axis=0)


def inv_rms(x):
    return lax.rsqrt(jnp.mean(x * x, axis=-1, keepdims=True) + EPS)


def pullback(x, gain, cotangent):
    rs = inv_rms(x)
    scaled = cotangent * gain
    along = jnp.mean(scaled * x, axis=-1, keepdims=True)
    return rs * scaled - x * (rs * rs * rs * along)


def kernel(
    window, q_ref, k_ref, v_ref, g_ref, gain_q, gain_k,
    gq_out, gk_out, gv_out,
    kv, qd, qdt, ktr, acc, dqt, part, part_in, total,
    col_out, col_in, row_out, row_in, dq_out, dq_in,
    ssem, rsem, lsem,
):
    me = lax.axis_index("head")
    tile = lax.axis_index("tile")
    frame = tile // PLANE
    row = tile // TC % TR
    col = tile % TC
    has_prev, has_next = frame > 0, frame < TF - 1
    has_left, has_right = col > 0, col < TC - 1
    partner = tile + TC * (1 - 2 * row)

    frame_to = (tile + PLANE, tile - PLANE)
    frame_sends = (has_next, has_prev)
    frame_gets = (has_prev, has_next)
    col_to = (tile + 1, tile - 1)
    col_sends = (has_right, has_left)
    col_gets = (has_left, has_right)

    started = []

    def remote(head, index, src, dst, axis, device):
        return pltpu.make_async_remote_copy(
            src_ref=src,
            dst_ref=dst,
            send_sem=ssem.at[head, index],
            recv_sem=rsem.at[head, index],
            device_id={axis: device},
            device_id_type=MESH,
        )

    def under(cond, fn):
        if cond is None:
            fn()
        else:
            pl.when(cond)(fn)

    def send(head, index, src, dst, device, cond=None):
        under(cond, lambda: remote(head, index, src, dst, "tile", device).start())
        started.append((cond, lambda: remote(head, index, src, dst, "tile", device).wait_send()))

    def arrive(head, index, dst, cond=None):
        under(cond, lambda: remote(head, index, dst, dst, "tile", partner).wait_recv())

    barrier = pltpu.get_barrier_semaphore()

    def greet(axis, device):
        pl.semaphore_signal(barrier, inc=1, device_id={axis: device}, device_id_type=MESH)

    for step in range(1, GROUP):
        greet("head", lax.rem(me + step, GROUP))
    greet("tile", partner)
    for slot in range(2):
        under(frame_sends[slot], lambda slot=slot: greet("tile", frame_to[slot]))
        under(col_sends[slot], lambda slot=slot: greet("tile", col_to[slot]))

    for head in range(2):
        lanes = pl.ds(head * HS, HS)
        x = k_ref[0, :, lanes].astype(jnp.float32)
        kv[head, 0, 1, 0] = (x * inv_rms(x) * gain_k[...]).astype(jnp.bfloat16)
        kv[head, 0, 1, 1] = v_ref[0, :, lanes]
        x = q_ref[0, :, lanes].astype(jnp.float32)
        qd[head, 1, 0] = (x * inv_rms(x) * gain_q[...]).astype(jnp.bfloat16)

    def clear(ref):
        ref[...] = jnp.zeros(ref.shape, ref.dtype)

    for slot in range(2):
        def no_frame(slot=slot):
            for head in range(2):
                clear(qd.at[head, 2 * slot])
                clear(part_in.at[head, slot])
                clear(total.at[head, 2 * slot])
                clear(dq_in.at[head, slot])

        def no_col(slot=slot):
            for head in range(2):
                for rr in range(2):
                    clear(kv.at[head, rr, 2 * slot])
                    clear(col_in.at[head, rr, slot])

        pl.when(jnp.logical_not(frame_gets[slot]))(no_frame)
        pl.when(jnp.logical_not(col_gets[slot]))(no_col)

    greeted = GROUP - 1 + 1
    for cond in (has_prev, has_next, has_left, has_right):
        greeted = greeted + jnp.where(cond, 1, 0)
    pl.semaphore_wait(barrier, greeted)

    def a2a(head, step):
        to = lax.rem(me + step, GROUP)
        src = g_ref.at[0, :, pl.ds(pl.multiple_of(to * (2 * HS) + head * HS, HS), HS)]
        dst = qd.at[head, 1, 1, pl.ds(pl.multiple_of(me * PIECE, 16), PIECE), :]
        return remote(head, A2A + step, src, dst, "head", to)

    def own_piece(head):
        src = g_ref.at[0, :, pl.ds(pl.multiple_of(me * (2 * HS) + head * HS, HS), HS)]
        dst = qd.at[head, 1, 1, pl.ds(pl.multiple_of(me * PIECE, 16), PIECE), :]
        return pltpu.make_async_copy(src, dst, lsem.at[head])

    def start_a2a(head):
        for step in range(1, GROUP):
            a2a(head, step).start()
            started.append((None, lambda step=step: a2a(head, step).wait_send()))
        own_piece(head).start()

    def end_a2a(head):
        for step in range(1, GROUP):
            come = lax.rem(me + GROUP - step, GROUP)
            dst = qd.at[head, 1, 1, pl.ds(pl.multiple_of(come * PIECE, 16), PIECE), :]
            remote(head, A2A + step, dst, dst, "head", come).wait_recv()
        own_piece(head).wait()

    def kv_row(head):
        send(head, KVROW, kv.at[head, 0, 1], kv.at[head, 1, 1], partner)

    def kv_cols(head, rr):
        for slot in range(2):
            send(
                head, KVCOL + 2 * rr + slot, kv.at[head, rr, 1], kv.at[head, rr, 2 * slot],
                col_to[slot], col_sends[slot],
            )

    def frames(head, base, kind):
        for slot in range(2):
            send(
                head, base + slot, qd.at[head, 1, kind], qd.at[head, 2 * slot, kind],
                frame_to[slot], frame_sends[slot],
            )

    def gather_first(head):
        kv_row(head)
        kv_cols(head, 0)
        frames(head, QF, 0)

    def gather_second(head):
        end_a2a(head)
        frames(head, DOF, 1)
        arrive(head, KVROW, kv.at[head, 1, 1])
        kv_cols(head, 1)

    def gather_end(head):
        for slot in range(2):
            arrive(head, QF + slot, qd.at[head, 2 * slot, 0], frame_gets[slot])
            arrive(head, DOF + slot, qd.at[head, 2 * slot, 1], frame_gets[slot])
            for rr in range(2):
                arrive(head, KVCOL + 2 * rr + slot, kv.at[head, rr, 2 * slot], col_gets[slot])

    def one_if(cond):
        return jnp.where(cond, 1, 0)

    def frame_mask(head, ff):
        if ff == 1:
            return 1
        if ff == 0:
            return window[head, 1] * one_if(has_prev)
        return -window[head, 0] * one_if(has_next)

    def row_mask(head, rr):
        other = jnp.where(row == 0, window[head, 3], -window[head, 2])
        return jnp.where(rr == 0, 1, other)

    def col_mask(head, cc):
        left = -window[head, 4] * one_if(has_left)
        right = window[head, 5] * one_if(has_right)
        return jnp.where(cc == 0, left, jnp.where(cc == 2, right, 1))

    def first_pass(head):
        for ff in range(3):
            for kind in range(2):
                qdt[head, ff, kind] = qd[head, ff, kind].T

        def body(i, carry):
            rr, cc = i // 3, i % 3
            keys, values = kv[head, rr, cc, 0], kv[head, rr, cc, 1]
            ktr[head, rr, cc] = keys.T
            place = row_mask(head, rr) * col_mask(head, cc)
            out = []
            for ff in range(3):
                live = jnp.where(place * frame_mask(head, ff) == 1, 1.0, 0.0)
                unnorm = jnp.exp2(dot(keys, qdt[head, ff, 0]) * EXP_SCALE)
                dprobs = dot(values, qdt[head, ff, 1])
                out.append(carry[2 * ff] + fold8(unnorm) * live)
                out.append(carry[2 * ff + 1] + fold8(unnorm * dprobs) * live)
            return tuple(out)

        zero = jnp.zeros((8, ROWS), jnp.float32)
        sums = lax.fori_loop(0, 6, body, (zero,) * 6)
        for ff in range(3):
            for at in range(2):
                part[head, ff, at : at + 1] = jnp.sum(sums[2 * ff + at], axis=0, keepdims=True)
            part[head, ff, 2:8] = jnp.zeros((6, ROWS), jnp.float32)

    def send_parts(head):
        for slot in range(2):
            send(
                head, PART + slot, part.at[head, 2 - 2 * slot], part_in.at[head, slot],
                frame_to[slot], frame_sends[slot],
            )

    def totals(head):
        for slot in range(2):
            arrive(head, PART + slot, part_in.at[head, slot], frame_gets[slot])
        both = part[head, 1, 0:2] + part_in[head, 0, 0:2] + part_in[head, 1, 0:2]
        total[head, 1, 0:1] = jnp.log(both[0:1]) * LOG2E
        total[head, 1, 1:2] = both[1:2] / both[0:1]
        total[head, 1, 2:8] = jnp.zeros((6, ROWS), jnp.float32)
        for slot in range(2):
            send(
                head, TOTAL + slot, total.at[head, 1], total.at[head, 2 * slot],
                frame_to[slot], frame_sends[slot],
            )

    def end_totals(head):
        for slot in range(2):
            arrive(head, TOTAL + slot, total.at[head, 2 * slot], frame_gets[slot])

    def second_pass(head):
        for ff in range(3):
            dqt[head, ff] = jnp.zeros((HS, ROWS), jnp.float32)

        def body(i, carry):
            own = i >= 4
            rr = jnp.where(own, 5 - i, 1 - i // 2)
            side = i % 2
            cc = jnp.where(own, 1, 2 * side)
            keys, values = kv[head, rr, cc, 0], kv[head, rr, cc, 1]
            keys_t = ktr[head, rr, cc]
            place = row_mask(head, rr) * col_mask(head, cc)
            dkey = jnp.zeros((ROWS, HS), jnp.float32)
            dvalue = jnp.zeros((ROWS, HS), jnp.float32)
            for ff in range(3):
                hide = jnp.where(place * frame_mask(head, ff) == 1, 0.0, HIDE)
                shift = total[head, ff, 0:1] + hide
                centre = total[head, ff, 1:2]
                probs = jnp.exp2(dot(keys, qdt[head, ff, 0]) * EXP_SCALE - shift)
                dprobs = dot(values, qdt[head, ff, 1])
                dscore = (probs * (dprobs - centre)).astype(jnp.bfloat16)
                dvalue = dvalue + dot(probs.astype(jnp.bfloat16), qd[head, ff, 1])
                dkey = dkey + dot(dscore, qd[head, ff, 0])
                dqt[head, ff] += dot(keys_t, dscore)
            dkey = dkey * SCALE

            def keep():
                acc[head, rr, 0] = dkey
                acc[head, rr, 1] = dvalue

            def give():
                col_out[head, rr, side, 0] = dkey.astype(jnp.bfloat16)
                col_out[head, rr, side, 1] = dvalue.astype(jnp.bfloat16)
                to_left = side == 0

                def go():
                    remote(
                        head, GCOL + 2 * rr + (1 - side), col_out.at[head, rr, side],
                        col_in.at[head, rr, 1 - side], "tile", tile + 2 * side - 1,
                    ).start()

                pl.when(jnp.logical_or(
                    jnp.logical_and(to_left, has_left),
                    jnp.logical_and(jnp.logical_not(to_left), has_right),
                ))(go)

            pl.when(own)(keep)
            pl.when(jnp.logical_not(own))(give)
            return carry

        lax.fori_loop(0, 6, body, 0)
        for rr in range(2):
            for slot in range(2):
                started.append((
                    col_sends[slot],
                    lambda rr=rr, slot=slot: remote(
                        head, GCOL + 2 * rr + slot, col_out.at[head, rr, 1 - slot],
                        col_in.at[head, rr, slot], "tile", col_to[slot],
                    ).wait_send(),
                ))

    def send_grads(head):
        for slot in range(2):
            arrive(head, GCOL + 2 + slot, col_in.at[head, 1, slot], col_gets[slot])
        for kind in range(2):
            summed = (
                acc[head, 1, kind]
                + col_in[head, 1, 0, kind].astype(jnp.float32)
                + col_in[head, 1, 1, kind].astype(jnp.float32)
            )
            row_out[head, kind] = summed.astype(jnp.bfloat16)
        send(head, GROW, row_out.at[head], row_in.at[head], partner)
        for slot in range(2):
            dq_out[head, slot] = (dqt[head, 2 - 2 * slot] * SCALE).T.astype(jnp.bfloat16)
            send(
                head, GQ + slot, dq_out.at[head, slot], dq_in.at[head, slot],
                frame_to[slot], frame_sends[slot],
            )

    def finish(head):
        lanes = pl.ds(head * HS, HS)
        for slot in range(2):
            arrive(head, GCOL + slot, col_in.at[head, 0, slot], col_gets[slot])
        arrive(head, GROW, row_in.at[head])
        sums = []
        for kind in range(2):
            sums.append(
                acc[head, 0, kind]
                + col_in[head, 0, 0, kind].astype(jnp.float32)
                + col_in[head, 0, 1, kind].astype(jnp.float32)
                + row_in[head, kind].astype(jnp.float32)
            )
        gk_out[0, :, lanes] = pullback(
            k_ref[0, :, lanes].astype(jnp.float32), gain_k[...], sums[0]
        ).astype(jnp.bfloat16)
        gv_out[0, :, lanes] = sums[1].astype(jnp.bfloat16)
        for slot in range(2):
            arrive(head, GQ + slot, dq_in.at[head, slot], frame_gets[slot])
        dquery = (
            (dqt[head, 1] * SCALE).T
            + dq_in[head, 0].astype(jnp.float32)
            + dq_in[head, 1].astype(jnp.float32)
        )
        gq_out[0, :, lanes] = pullback(
            q_ref[0, :, lanes].astype(jnp.float32), gain_q[...], dquery
        ).astype(jnp.bfloat16)

    start_a2a(0)
    gather_first(0)
    start_a2a(1)
    gather_second(0)
    gather_first(1)
    gather_end(0)
    first_pass(0)
    send_parts(0)
    gather_second(1)
    totals(0)
    end_totals(0)
    second_pass(0)
    send_grads(0)
    gather_end(1)
    first_pass(1)
    send_parts(1)
    totals(1)
    end_totals(1)
    second_pass(1)
    send_grads(1)
    finish(0)
    finish(1)
    for cond, wait in started:
        under(cond, wait)


def shards(query, key, value, grad_out, gain_q, gain_k, window):
    half = jax.ShapeDtypeStruct(query.shape, jnp.bfloat16)
    vmem = pl.BlockSpec(memory_space=pltpu.VMEM)
    low, full = jnp.bfloat16, jnp.float32
    return pl.pallas_call(
        kernel,
        out_shape=(half, half, half),
        in_specs=[pl.BlockSpec(memory_space=pltpu.SMEM)] + [vmem] * 6,
        out_specs=(vmem, vmem, vmem),
        scratch_shapes=[
            pltpu.VMEM((2, 2, 3, 2, ROWS, HS), low),
            pltpu.VMEM((2, 3, 2, ROWS, HS), low),
            pltpu.VMEM((2, 3, 2, HS, ROWS), low),
            pltpu.VMEM((2, 2, 3, HS, ROWS), low),
            pltpu.VMEM((2, 2, 2, ROWS, HS), full),
            pltpu.VMEM((2, 3, HS, ROWS), full),
            pltpu.VMEM((2, 3, 8, ROWS), full),
            pltpu.VMEM((2, 2, 8, ROWS), full),
            pltpu.VMEM((2, 3, 8, ROWS), full),
            pltpu.VMEM((2, 2, 2, 2, ROWS, HS), low),
            pltpu.VMEM((2, 2, 2, 2, ROWS, HS), low),
            pltpu.VMEM((2, 2, ROWS, HS), low),
            pltpu.VMEM((2, 2, ROWS, HS), low),
            pltpu.VMEM((2, 2, ROWS, HS), low),
            pltpu.VMEM((2, 2, ROWS, HS), low),
            pltpu.SemaphoreType.DMA((2, COPIES)),
            pltpu.SemaphoreType.DMA((2, COPIES)),
            pltpu.SemaphoreType.DMA((2,)),
        ],
        compiler_params=pltpu.CompilerParams(
            collective_id=0, has_side_effects=True, vmem_limit_bytes=56 * 1024 * 1024
        ),
    )(window, query, key, value, grad_out, gain_q.reshape(1, HS), gain_k.reshape(1, HS))


def solution(mesh):
    placed = (
        P("tile", None, "head"),
        P("tile", None, "head"),
        P("tile", None, "head"),
        P("tile", "head", None),
        P(),
        P(),
        P("head", None),
    )
    return jax.shard_map(
        shards,
        mesh=mesh,
        in_specs=placed,
        out_specs=(P("tile", None, "head"), P("tile", None, "head"), P("tile", None, "head")),
        check_vma=False,
    )
```

```python
import math

import jax
import jax.numpy as jnp
from jax import lax
from jax.experimental import pallas as pl
from jax.experimental.pallas import tpu as pltpu
from jax.sharding import PartitionSpec as P

MESH = pl.DeviceIdType.MESH
HS = 128
TF, TR, TC = 4, 2, 4
ROWS = 384
PIECE = 48
GROUP = 8
PLANE = TR * TC
SCALE = 1.0 / math.sqrt(HS)
EXP_SCALE = SCALE * math.log2(math.e)
EPS = 1e-6

A2A = 0
KVROW = 8
KVCOL = 9
QF = 13
DOF = 15
PART = 17
TOTAL = 19
GCOL = 21
GROW = 25
GQ = 26
COPIES = 28


def dot(a, b):
    return jnp.dot(a, b, preferred_element_type=jnp.float32)


def fold8(x):
    return jnp.sum(x.reshape(x.shape[0] // 8, 8, x.shape[1]), axis=0)


def inv_rms(x):
    return lax.rsqrt(jnp.mean(x * x, axis=-1, keepdims=True) + EPS)


def pullback(x, gain, cotangent):
    rs = inv_rms(x)
    scaled = cotangent * gain
    along = jnp.mean(scaled * x, axis=-1, keepdims=True)
    return rs * scaled - x * (rs * rs * rs * along)


def kernel(
    window, q_hbm, k_hbm, v_hbm, g_ref, gain_q, gain_k,
    dq_sum, dk_sum, dv_sum,
    q_ref, k_ref, v_ref,
    kv, qd, qdt, ktr, acc, dqt, part, part_in, total,
    col_out, col_in, row_out, row_in, dq_out, dq_in, unnorm_kept, dprobs_kept,
    ssem, rsem, lsem,
):
    me = lax.axis_index("head")
    tile = lax.axis_index("tile")
    frame = tile // PLANE
    row = tile // TC % TR
    col = tile % TC
    has_prev, has_next = frame > 0, frame < TF - 1
    has_left, has_right = col > 0, col < TC - 1
    partner = tile + TC * (1 - 2 * row)

    has_remote = jnp.where(row == 0, frame, TF - 1 - frame) > 0
    site = (tile - TC * (1 + row), tile + TC * (2 - row))
    has_site = (has_prev, has_next)
    owner = tuple(tile + TC * (3 * row - 2 + j) for j in range(2))
    my_side = 1 - row

    col_to = (tile + 1, tile - 1)
    col_sends = (has_right, has_left)
    col_gets = (has_left, has_right)

    started = []

    def remote(head, index, src, dst, axis, device, got=None):
        return pltpu.make_async_remote_copy(
            src_ref=src,
            dst_ref=dst,
            send_sem=ssem.at[head, index],
            recv_sem=rsem.at[head, index if got is None else got],
            device_id={axis: device},
            device_id_type=MESH,
        )

    def under(cond, fn):
        if cond is None:
            fn()
        else:
            pl.when(cond)(fn)

    def send(head, index, src, dst, device, cond=None, got=None):
        def copy():
            return remote(head, index, src, dst, "tile", device, got)

        under(cond, lambda: copy().start())
        started.append((cond, lambda: copy().wait_send()))

    def arrive(head, index, dst, cond=None):
        under(cond, lambda: remote(head, index, dst, dst, "tile", partner).wait_recv())

    barrier = pltpu.get_barrier_semaphore()

    def greet(axis, device):
        pl.semaphore_signal(barrier, inc=1, device_id={axis: device}, device_id_type=MESH)

    for step in range(1, GROUP):
        greet("head", lax.rem(me + step, GROUP))
    near = (
        (tile - TC, tile >= TC),
        (tile + TC, tile < TF * PLANE - TC),
        (tile - 2 * TC, has_prev),
        (tile + 2 * TC, has_next),
        (tile - 1, has_left),
        (tile + 1, has_right),
    )
    for device, cond in near:
        under(cond, lambda device=device: greet("tile", device))

    loads = [
        pltpu.make_async_copy(src, dst, lsem.at[2 + at])
        for at, (src, dst) in enumerate(((k_hbm, k_ref), (v_hbm, v_ref), (q_hbm, q_ref)))
    ]
    for load in loads:
        load.start()
    for load in loads:
        load.wait()

    for head in range(2):
        lanes = pl.ds(head * HS, HS)
        x = k_ref[0, :, lanes].astype(jnp.float32)
        kv[head, 0, 1, 0] = (x * inv_rms(x) * gain_k[...]).astype(jnp.bfloat16)
        kv[head, 0, 1, 1] = v_ref[0, :, lanes]
        x = q_ref[0, :, lanes].astype(jnp.float32)
        qd[head, 1, 0] = (x * inv_rms(x) * gain_q[...]).astype(jnp.bfloat16)

    def clear(ref):
        ref[...] = jnp.zeros(ref.shape, ref.dtype)

    def no_remote():
        for head in range(2):
            for j in range(2):
                clear(qd.at[head, 2 * j])
                clear(total.at[head, 2 * j])

    pl.when(jnp.logical_not(has_remote))(no_remote)

    for slot in range(2):
        def no_site(slot=slot):
            for head in range(2):
                clear(part_in.at[head, slot])
                clear(dq_in.at[head, slot])

        def no_col(slot=slot):
            for head in range(2):
                for rr in range(2):
                    clear(kv.at[head, rr, 2 * slot])
                    clear(col_in.at[head, rr, slot])

        pl.when(jnp.logical_not(has_site[slot]))(no_site)
        pl.when(jnp.logical_not(col_gets[slot]))(no_col)

    greeted = GROUP - 1
    for _, cond in near:
        greeted = greeted + jnp.where(cond, 1, 0)
    pl.semaphore_wait(barrier, greeted)

    def a2a(head, step):
        to = lax.rem(me + step, GROUP)
        src = g_ref.at[0, :, pl.ds(pl.multiple_of(to * (2 * HS) + head * HS, HS), HS)]
        dst = qd.at[head, 1, 1, pl.ds(pl.multiple_of(me * PIECE, 16), PIECE), :]
        return remote(head, A2A + step, src, dst, "head", to)

    def own_piece(head):
        src = g_ref.at[0, :, pl.ds(pl.multiple_of(me * (2 * HS) + head * HS, HS), HS)]
        dst = qd.at[head, 1, 1, pl.ds(pl.multiple_of(me * PIECE, 16), PIECE), :]
        return pltpu.make_async_copy(src, dst, lsem.at[head])

    def start_a2a(head):
        for step in range(1, GROUP):
            a2a(head, step).start()
            started.append((None, lambda step=step: a2a(head, step).wait_send()))
        own_piece(head).start()

    def end_a2a(head):
        for step in range(1, GROUP):
            come = lax.rem(me + GROUP - step, GROUP)
            dst = qd.at[head, 1, 1, pl.ds(pl.multiple_of(come * PIECE, 16), PIECE), :]
            remote(head, A2A + step, dst, dst, "head", come).wait_recv()
        own_piece(head).wait()

    def kv_row(head):
        send(head, KVROW, kv.at[head, 0, 1], kv.at[head, 1, 1], partner)

    def kv_cols(head, rr):
        for slot in range(2):
            send(
                head, KVCOL + 2 * rr + slot, kv.at[head, rr, 1], kv.at[head, rr, 2 * slot],
                col_to[slot], col_sends[slot],
            )

    def to_sites(head, base, src, dst):
        for side in range(2):
            send(head, base + side, src, dst, site[side], has_site[side], base + row)

    def to_owners(head, base, srcs, dst):
        for j in range(2):
            send(head, base + j, srcs.at[head, j], dst, owner[j], has_remote, base + my_side)

    def frames(head, base, kind):
        to_sites(head, base, qd.at[head, 1, kind], qd.at[head, 2 * row, kind])

    def gather_first(head):
        kv_row(head)
        kv_cols(head, 0)
        frames(head, QF, 0)

    def cotangents(head):
        end_a2a(head)
        frames(head, DOF, 1)

    def forward_row(head):
        arrive(head, KVROW, kv.at[head, 1, 1])
        kv_cols(head, 1)

    def end_cols(head):
        for slot in range(2):
            for rr in range(2):
                arrive(head, KVCOL + 2 * rr + slot, kv.at[head, rr, 2 * slot], col_gets[slot])

    def end_frames(head):
        for j in range(2):
            arrive(head, QF + j, qd.at[head, 2 * j, 0], has_remote)
            arrive(head, DOF + j, qd.at[head, 2 * j, 1], has_remote)

    def one_if(cond):
        return jnp.where(cond, 1, 0)

    def query_mask(head, ff, rr):
        key_row = jnp.where(rr == 0, row, 1 - row)
        offset = key_row - (0, row, 1)[ff]
        rows = jnp.where(offset == 0, 1, jnp.where(offset > 0, window[head, 3], -window[head, 2]))
        if ff == 1:
            return rows
        frames = jnp.where(row == 0, window[head, 1], -window[head, 0])
        return rows * frames * one_if(has_remote)

    def col_mask(head, cc):
        left = -window[head, 4] * one_if(has_left)
        right = window[head, 5] * one_if(has_right)
        return jnp.where(cc == 0, left, jnp.where(cc == 2, right, 1))

    def first_pass(head, ffs):
        for ff in ffs:
            for kind in range(2):
                qdt[head, ff, kind] = qd[head, ff, kind].T

        def body(i, carry):
            rr, cc = i // 3, i % 3
            keys, values = kv[head, rr, cc, 0], kv[head, rr, cc, 1]
            if 1 in ffs:
                ktr[head, rr, cc] = keys.T
            place = col_mask(head, cc)
            out = []
            for at, ff in enumerate(ffs):
                live = jnp.where(place * query_mask(head, ff, rr) == 1, 1.0, 0.0)
                unnorm = jnp.exp2(dot(keys, qdt[head, ff, 0]) * EXP_SCALE)
                dprobs = dot(values, qdt[head, ff, 1])
                unnorm_kept[head, rr, cc, ff] = unnorm.astype(jnp.bfloat16)
                dprobs_kept[head, rr, cc, ff] = dprobs
                out.append(carry[2 * at] + fold8(unnorm) * live)
                out.append(carry[2 * at + 1] + fold8(unnorm * dprobs) * live)
            return tuple(out)

        zero = jnp.zeros((8, ROWS), jnp.float32)
        sums = lax.fori_loop(0, 6, body, (zero,) * (2 * len(ffs)))
        for at, ff in enumerate(ffs):
            for kind in range(2):
                part[head, ff, kind : kind + 1] = jnp.sum(
                    sums[2 * at + kind], axis=0, keepdims=True
                )
            part[head, ff, 2:8] = jnp.zeros((6, ROWS), jnp.float32)

    def send_parts(head):
        for j in range(2):
            send(
                head, PART + j, part.at[head, 2 * j], part_in.at[head, my_side],
                owner[j], has_remote, PART + my_side,
            )

    def totals(head):
        for slot in range(2):
            arrive(head, PART + slot, part_in.at[head, slot], has_site[slot])
        both = part[head, 1, 0:2] + part_in[head, 0, 0:2] + part_in[head, 1, 0:2]
        total[head, 1, 0:1] = 1.0 / both[0:1]
        total[head, 1, 1:2] = both[1:2] / both[0:1]
        total[head, 1, 2:8] = jnp.zeros((6, ROWS), jnp.float32)
        to_sites(head, TOTAL, total.at[head, 1], total.at[head, 2 * row])

    def end_totals(head):
        for j in range(2):
            arrive(head, TOTAL + j, total.at[head, 2 * j], has_remote)

    def key_tile(head, rr, cc):
        keys_t = ktr[head, rr, cc]
        place = col_mask(head, cc)
        dkey = jnp.zeros((ROWS, HS), jnp.float32)
        dvalue = jnp.zeros((ROWS, HS), jnp.float32)
        for ff in range(3):
            live = jnp.where(place * query_mask(head, ff, rr) == 1, 1.0, 0.0)
            share = total[head, ff, 0:1] * live
            centre = total[head, ff, 1:2]
            probs = unnorm_kept[head, rr, cc, ff].astype(jnp.float32) * share
            dscore = (probs * (dprobs_kept[head, rr, cc, ff] - centre)).astype(jnp.bfloat16)
            dvalue = dvalue + dot(probs.astype(jnp.bfloat16), qd[head, ff, 1])
            dkey = dkey + dot(dscore, qd[head, ff, 0])
            dqt[head, ff] += dot(keys_t, dscore)
        return dkey * SCALE, dvalue

    def grads_cols(head):
        for ff in range(3):
            dqt[head, ff] = jnp.zeros((HS, ROWS), jnp.float32)

        def body(i, carry):
            rr = 1 - i // 2
            side = i % 2
            dkey, dvalue = key_tile(head, rr, 2 * side)
            col_out[head, rr, side, 0] = dkey.astype(jnp.bfloat16)
            col_out[head, rr, side, 1] = dvalue.astype(jnp.bfloat16)

            def go():
                remote(
                    head, GCOL + 2 * rr + (1 - side), col_out.at[head, rr, side],
                    col_in.at[head, rr, 1 - side], "tile", tile + 2 * side - 1,
                ).start()

            pl.when(jnp.where(side == 0, one_if(has_left), one_if(has_right)) == 1)(go)
            return carry

        lax.fori_loop(0, 4, body, 0)
        for rr in range(2):
            for slot in range(2):
                started.append((
                    col_sends[slot],
                    lambda rr=rr, slot=slot: remote(
                        head, GCOL + 2 * rr + slot, col_out.at[head, rr, 1 - slot],
                        col_in.at[head, rr, slot], "tile", col_to[slot],
                    ).wait_send(),
                ))

    def grads_own(head, rr):
        acc[head, rr, 0], acc[head, rr, 1] = key_tile(head, rr, 1)

    def send_row(head):
        for slot in range(2):
            arrive(head, GCOL + 2 + slot, col_in.at[head, 1, slot], col_gets[slot])
        for kind in range(2):
            summed = (
                acc[head, 1, kind]
                + col_in[head, 1, 0, kind].astype(jnp.float32)
                + col_in[head, 1, 1, kind].astype(jnp.float32)
            )
            row_out[head, kind] = summed.astype(jnp.bfloat16)
        send(head, GROW, row_out.at[head], row_in.at[head], partner)

    def send_queries(head):
        for j in range(2):
            dq_out[head, j] = (dqt[head, 2 * j] * SCALE).T.astype(jnp.bfloat16)
        to_owners(head, GQ, dq_out, dq_in.at[head, my_side])

    def finish(head):
        lanes = pl.ds(head * HS, HS)
        for slot in range(2):
            arrive(head, GCOL + slot, col_in.at[head, 0, slot], col_gets[slot])
        arrive(head, GROW, row_in.at[head])
        sums = []
        for kind in range(2):
            sums.append(
                acc[head, 0, kind]
                + col_in[head, 0, 0, kind].astype(jnp.float32)
                + col_in[head, 0, 1, kind].astype(jnp.float32)
                + row_in[head, kind].astype(jnp.float32)
            )
        dk_sum[0, :, lanes] = sums[0]
        dv_sum[0, :, lanes] = sums[1].astype(jnp.bfloat16)
        for slot in range(2):
            arrive(head, GQ + slot, dq_in.at[head, slot], has_site[slot])
        dq_sum[0, :, lanes] = (
            (dqt[head, 1] * SCALE).T
            + dq_in[head, 0].astype(jnp.float32)
            + dq_in[head, 1].astype(jnp.float32)
        )

    start_a2a(0)
    gather_first(0)
    start_a2a(1)
    cotangents(0)
    forward_row(0)
    gather_first(1)
    cotangents(1)
    end_cols(0)
    first_pass(0, (1,))
    end_frames(0)
    first_pass(0, (0, 2))
    send_parts(0)
    forward_row(1)
    end_cols(1)
    first_pass(1, (1,))
    totals(0)
    end_frames(1)
    first_pass(1, (0, 2))
    send_parts(1)
    end_totals(0)
    grads_cols(0)
    totals(1)
    grads_own(0, 1)
    send_row(0)
    grads_own(0, 0)
    send_queries(0)
    end_totals(1)
    grads_cols(1)
    grads_own(1, 1)
    send_row(1)
    grads_own(1, 0)
    send_queries(1)
    finish(0)
    finish(1)
    for cond, wait in started:
        under(cond, wait)


def pull_kernel(q_ref, k_ref, dq_ref, dk_ref, dv_ref, gain_q, gain_k, gq_out, gk_out, gv_out):
    for head in range(2):
        lanes = pl.ds(head * HS, HS)
        for x_ref, d_ref, gain, out in (
            (q_ref, dq_ref, gain_q, gq_out),
            (k_ref, dk_ref, gain_k, gk_out),
        ):
            x = x_ref[0, :, lanes].astype(jnp.float32)
            out[0, :, lanes] = pullback(x, gain[...], d_ref[0, :, lanes]).astype(jnp.bfloat16)
    gv_out[...] = dv_ref[...]


def shards(query, key, value, grad_out, gain_q, gain_k, window):
    half = jax.ShapeDtypeStruct(query.shape, jnp.bfloat16)
    wide = jax.ShapeDtypeStruct(query.shape, jnp.float32)
    vmem = pl.BlockSpec(memory_space=pltpu.VMEM)
    anywhere = pl.BlockSpec(memory_space=pl.ANY)
    low, full = jnp.bfloat16, jnp.float32
    gain_q, gain_k = gain_q.reshape(1, HS), gain_k.reshape(1, HS)
    dquery, dkey, dvalue = pl.pallas_call(
        kernel,
        out_shape=(wide, wide, half),
        in_specs=[pl.BlockSpec(memory_space=pltpu.SMEM)] + [anywhere] * 4 + [vmem] * 2,
        out_specs=(vmem, vmem, vmem),
        scratch_shapes=[
            pltpu.VMEM(query.shape, low),
            pltpu.VMEM(query.shape, low),
            pltpu.VMEM(query.shape, low),
            pltpu.VMEM((2, 2, 3, 2, ROWS, HS), low),
            pltpu.VMEM((2, 3, 2, ROWS, HS), low),
            pltpu.VMEM((2, 3, 2, HS, ROWS), low),
            pltpu.VMEM((2, 2, 3, HS, ROWS), low),
            pltpu.VMEM((2, 2, 2, ROWS, HS), full),
            pltpu.VMEM((2, 3, HS, ROWS), full),
            pltpu.VMEM((2, 3, 8, ROWS), full),
            pltpu.VMEM((2, 2, 8, ROWS), full),
            pltpu.VMEM((2, 3, 8, ROWS), full),
            pltpu.VMEM((2, 2, 2, 2, ROWS, HS), low),
            pltpu.VMEM((2, 2, 2, 2, ROWS, HS), low),
            pltpu.VMEM((2, 2, ROWS, HS), low),
            pltpu.VMEM((2, 2, ROWS, HS), low),
            pltpu.VMEM((2, 2, ROWS, HS), low),
            pltpu.VMEM((2, 2, ROWS, HS), low),
            pltpu.VMEM((2, 2, 3, 3, ROWS, ROWS), low),
            pltpu.VMEM((2, 2, 3, 3, ROWS, ROWS), full),
            pltpu.SemaphoreType.DMA((2, COPIES)),
            pltpu.SemaphoreType.DMA((2, COPIES)),
            pltpu.SemaphoreType.DMA((5,)),
        ],
        compiler_params=pltpu.CompilerParams(
            collective_id=0, has_side_effects=True, vmem_limit_bytes=60 * 1024 * 1024
        ),
    )(window, query, key, value, grad_out, gain_q, gain_k)
    return pl.pallas_call(
        pull_kernel,
        out_shape=(half, half, half),
        in_specs=[vmem] * 7,
        out_specs=(vmem, vmem, vmem),
    )(query, key, dquery, dkey, dvalue, gain_q, gain_k)


def solution(mesh):
    placed = (
        P("tile", None, "head"),
        P("tile", None, "head"),
        P("tile", None, "head"),
        P("tile", "head", None),
        P(),
        P(),
        P("head", None),
    )
    return jax.shard_map(
        shards,
        mesh=mesh,
        in_specs=placed,
        out_specs=(P("tile", None, "head"), P("tile", None, "head"), P("tile", None, "head")),
        check_vma=False,
    )
```

```python
import math

import jax
import jax.numpy as jnp
from jax import lax
from jax.experimental import pallas as pl
from jax.experimental.pallas import tpu as pltpu
from jax.sharding import PartitionSpec as P

MESH = pl.DeviceIdType.MESH
HS = 128
TF, TR, TC = 4, 2, 4
ROWS = 384
PIECE = 48
GROUP = 8
PLANE = TR * TC
SCALE = 1.0 / math.sqrt(HS)
EXP_SCALE = SCALE * math.log2(math.e)
EPS = 1e-6

A2A = 0
KVROW = 8
KVCOL = 9
QF = 13
DOF = 15
PART = 17
OWNPART = 19
GCOL = 21
GROW = 25
GQ = 26
OPPOSITE = 28
COPIES = 29

OWN = 2


def dot(a, b):
    return jnp.dot(a, b, preferred_element_type=jnp.float32)


def fold8(x):
    return jnp.sum(x.reshape(x.shape[0] // 8, 8, x.shape[1]), axis=0)


def inv_rms(x):
    return lax.rsqrt(jnp.mean(x * x, axis=-1, keepdims=True) + EPS)


def pullback(x, gain, cotangent):
    rs = inv_rms(x)
    scaled = cotangent * gain
    along = jnp.mean(scaled * x, axis=-1, keepdims=True)
    return rs * scaled - x * (rs * rs * rs * along)


def kernel(
    window, q_hbm, k_hbm, v_hbm, g_ref, gain_q, gain_k,
    dq_sum, dk_sum, dv_sum,
    q_ref, k_ref, v_ref,
    kv, qd, qdt, ktr, acc, dqt, part, part_in, own_in, opp_in, total,
    col_out, col_in, row_out, row_in, dq_out, dq_in, unnorm_kept, dprobs_kept,
    ssem, rsem, lsem,
):
    me = lax.axis_index("head")
    tile = lax.axis_index("tile")
    frame = tile // PLANE
    row = tile // TC % TR
    col = tile % TC
    has_prev, has_next = frame > 0, frame < TF - 1
    has_left, has_right = col > 0, col < TC - 1
    partner = tile + TC * (1 - 2 * row)

    has_remote = jnp.where(row == 0, frame, TF - 1 - frame) > 0
    site = (tile - TC * (1 + row), tile + TC * (2 - row))
    has_site = (has_prev, has_next)
    owner = tuple(tile + TC * (3 * row - 2 + j) for j in range(2))
    my_side = 1 - row
    opposite = tile + 3 * TC * (2 * row - 1)
    has_opposite = jnp.where(row == 0, frame, TF - 1 - frame) > 1

    col_to = (tile + 1, tile - 1)
    col_sends = (has_right, has_left)
    col_gets = (has_left, has_right)

    started = []

    def remote(head, index, src, dst, axis, device, got=None):
        return pltpu.make_async_remote_copy(
            src_ref=src,
            dst_ref=dst,
            send_sem=ssem.at[head, index],
            recv_sem=rsem.at[head, index if got is None else got],
            device_id={axis: device},
            device_id_type=MESH,
        )

    def under(cond, fn):
        if cond is None:
            fn()
        else:
            pl.when(cond)(fn)

    def send(head, index, src, dst, device, cond=None, got=None):
        def copy():
            return remote(head, index, src, dst, "tile", device, got)

        under(cond, lambda: copy().start())
        started.append((cond, lambda: copy().wait_send()))

    def arrive(head, index, dst, cond=None):
        under(cond, lambda: remote(head, index, dst, dst, "tile", partner).wait_recv())

    barrier = pltpu.get_barrier_semaphore()

    def greet(axis, device):
        pl.semaphore_signal(barrier, inc=1, device_id={axis: device}, device_id_type=MESH)

    for step in range(1, GROUP):
        greet("head", lax.rem(me + step, GROUP))
    near = (
        (tile - TC, tile >= TC),
        (tile + TC, tile < TF * PLANE - TC),
        (tile - 2 * TC, has_prev),
        (tile + 2 * TC, has_next),
        (opposite, has_opposite),
        (tile - 1, has_left),
        (tile + 1, has_right),
    )
    for device, cond in near:
        under(cond, lambda device=device: greet("tile", device))

    loads = [
        pltpu.make_async_copy(src, dst, lsem.at[2 + at])
        for at, (src, dst) in enumerate(((k_hbm, k_ref), (v_hbm, v_ref), (q_hbm, q_ref)))
    ]
    for load in loads:
        load.start()
    for load in loads:
        load.wait()

    for head in range(2):
        lanes = pl.ds(head * HS, HS)
        x = k_ref[0, :, lanes].astype(jnp.float32)
        kv[head, 0, 1, 0] = (x * inv_rms(x) * gain_k[...]).astype(jnp.bfloat16)
        kv[head, 0, 1, 1] = v_ref[0, :, lanes]
        x = q_ref[0, :, lanes].astype(jnp.float32)
        qd[head, 0, OWN] = (x * inv_rms(x) * gain_q[...]).astype(jnp.bfloat16)

    def clear(ref):
        ref[...] = jnp.zeros(ref.shape, ref.dtype)

    def no_remote():
        for head in range(2):
            clear(total.at[head])
            for kind in range(2):
                clear(qd.at[head, kind, pl.ds(0, 2)])

    pl.when(jnp.logical_not(has_remote))(no_remote)

    def no_opposite():
        for head in range(2):
            clear(opp_in.at[head])

    pl.when(jnp.logical_not(has_opposite))(no_opposite)

    for slot in range(2):
        def no_site(slot=slot):
            for head in range(2):
                clear(part_in.at[head, slot])
                clear(dq_in.at[head, slot])

        def no_col(slot=slot):
            for head in range(2):
                for rr in range(2):
                    clear(kv.at[head, rr, 2 * slot])
                    clear(col_in.at[head, rr, slot])

        pl.when(jnp.logical_not(has_site[slot]))(no_site)
        pl.when(jnp.logical_not(col_gets[slot]))(no_col)

    greeted = GROUP - 1
    for _, cond in near:
        greeted = greeted + jnp.where(cond, 1, 0)
    pl.semaphore_wait(barrier, greeted)

    def a2a(head, step):
        to = lax.rem(me + step, GROUP)
        src = g_ref.at[0, :, pl.ds(pl.multiple_of(to * (2 * HS) + head * HS, HS), HS)]
        dst = qd.at[head, 1, OWN, pl.ds(pl.multiple_of(me * PIECE, 16), PIECE), :]
        return remote(head, A2A + step, src, dst, "head", to)

    def own_piece(head):
        src = g_ref.at[0, :, pl.ds(pl.multiple_of(me * (2 * HS) + head * HS, HS), HS)]
        dst = qd.at[head, 1, OWN, pl.ds(pl.multiple_of(me * PIECE, 16), PIECE), :]
        return pltpu.make_async_copy(src, dst, lsem.at[head])

    def start_a2a(head):
        for step in range(1, GROUP):
            a2a(head, step).start()
            started.append((None, lambda step=step: a2a(head, step).wait_send()))
        own_piece(head).start()

    def end_a2a(head):
        for step in range(1, GROUP):
            come = lax.rem(me + GROUP - step, GROUP)
            dst = qd.at[head, 1, OWN, pl.ds(pl.multiple_of(come * PIECE, 16), PIECE), :]
            remote(head, A2A + step, dst, dst, "head", come).wait_recv()
        own_piece(head).wait()

    def kv_row(head):
        send(head, KVROW, kv.at[head, 0, 1], kv.at[head, 1, 1], partner)

    def kv_cols(head, rr):
        for slot in range(2):
            send(
                head, KVCOL + 2 * rr + slot, kv.at[head, rr, 1], kv.at[head, rr, 2 * slot],
                col_to[slot], col_sends[slot],
            )

    def to_sites(head, base, src, dst):
        for side in range(2):
            send(head, base + side, src, dst, site[side], has_site[side], base + row)

    def to_owners(head, base, srcs, dst):
        for j in range(2):
            send(head, base + j, srcs.at[head, j], dst, owner[j], has_remote, base + my_side)

    def frames(head, base, kind):
        to_sites(head, base, qd.at[head, kind, OWN], qd.at[head, kind, row])

    def gather_first(head):
        kv_row(head)
        kv_cols(head, 0)
        frames(head, QF, 0)

    def cotangents(head):
        end_a2a(head)
        frames(head, DOF, 1)

    def forward_row(head):
        arrive(head, KVROW, kv.at[head, 1, 1])
        kv_cols(head, 1)

    def end_cols(head):
        for slot in range(2):
            for rr in range(2):
                arrive(head, KVCOL + 2 * rr + slot, kv.at[head, rr, 2 * slot], col_gets[slot])

    def end_frames(head):
        for j in range(2):
            arrive(head, QF + j, qd.at[head, 0, j], has_remote)
            arrive(head, DOF + j, qd.at[head, 1, j], has_remote)

    def one_if(cond):
        return jnp.where(cond, 1, 0)

    def query_mask(head, ff, rr):
        key_row = jnp.where(rr == 0, row, 1 - row)
        offset = key_row - (0, 1, row)[ff]
        rows = jnp.where(offset == 0, 1, jnp.where(offset > 0, window[head, 3], -window[head, 2]))
        if ff == OWN:
            return rows
        frames = jnp.where(row == 0, window[head, 1], -window[head, 0])
        return rows * frames * one_if(has_remote)

    def col_mask(head, cc):
        left = -window[head, 4] * one_if(has_left)
        right = window[head, 5] * one_if(has_right)
        return jnp.where(cc == 0, left, jnp.where(cc == 2, right, 1))

    def live(head, rr, cc, ff):
        return jnp.where(col_mask(head, cc) * query_mask(head, ff, rr) == 1, 1.0, 0.0)

    def first_pass(head, ffs):
        lanes = pl.ds(ffs[0] * ROWS, len(ffs) * ROWS)
        for ff in ffs:
            for kind in range(2):
                qdt[head, kind, :, pl.ds(ff * ROWS, ROWS)] = qd[head, kind, ff].T

        def body(i, carry):
            rr, cc = i // 3, i % 3
            keys, values = kv[head, rr, cc, 0], kv[head, rr, cc, 1]
            if OWN in ffs:
                ktr[head, rr, cc] = keys.T
            unnorm = jnp.exp2(dot(keys, qdt[head, 0, :, lanes]) * EXP_SCALE)
            dprobs = dot(values, qdt[head, 1, :, lanes])
            unnorm_kept[head, rr, cc, :, lanes] = unnorm.astype(jnp.bfloat16)
            dprobs_kept[head, rr, cc, :, lanes] = dprobs
            sums = (fold8(unnorm), fold8(unnorm * dprobs))
            out = []
            for at, ff in enumerate(ffs):
                here = live(head, rr, cc, ff)
                for kind in range(2):
                    mine = sums[kind][:, at * ROWS : (at + 1) * ROWS]
                    out.append(carry[2 * at + kind] + mine * here)
            return tuple(out)

        zero = jnp.zeros((8, ROWS), jnp.float32)
        sums = lax.fori_loop(0, 6, body, (zero,) * (2 * len(ffs)), unroll=6)
        for at, ff in enumerate(ffs):
            for kind in range(2):
                part[head, ff, kind : kind + 1] = jnp.sum(
                    sums[2 * at + kind], axis=0, keepdims=True
                )
            part[head, ff, 2:8] = jnp.zeros((6, ROWS), jnp.float32)

    def send_own_part(head):
        to_sites(head, OWNPART, part.at[head, OWN], own_in.at[head, row])

    def send_parts(head):
        to_owners(head, PART, part, part_in.at[head, my_side])
        send(
            head, OPPOSITE, part.at[head, pl.ds(0, 2)], opp_in.at[head], opposite, has_opposite
        )

    def totals(head):
        def put(ff, terms):
            both = part[head, ff, 0:2] + terms[0][0:2] + terms[1][0:2]
            lanes = pl.ds(ff * ROWS, ROWS)
            total[head, 0:1, lanes] = 1.0 / both[0:1]
            total[head, 1:2, lanes] = both[1:2] / both[0:1]

        for slot in range(2):
            arrive(head, PART + slot, part_in.at[head, slot], has_site[slot])
        put(OWN, (part_in[head, 0], part_in[head, 1]))
        for j in range(2):
            arrive(head, OWNPART + j, own_in.at[head, j], has_remote)
        arrive(head, OPPOSITE, opp_in.at[head], has_opposite)

        def put_remote():
            for j in range(2):
                put(j, (own_in[head, j], opp_in[head, j]))

        pl.when(has_remote)(put_remote)

    def key_tiles(head, places):
        queries = qd[head, 0].reshape(3 * ROWS, HS)
        cotangents = qd[head, 1].reshape(3 * ROWS, HS)
        centre = total[head, 1:2]
        out, scores = [], []
        for rr, cc in places:
            alive = jnp.concatenate(
                [jnp.full((1, ROWS), live(head, rr, cc, ff), jnp.float32) for ff in range(3)],
                axis=1,
            )
            share = total[head, 0:1] * alive
            probs = unnorm_kept[head, rr, cc].astype(jnp.float32) * share
            dscore = (probs * (dprobs_kept[head, rr, cc] - centre)).astype(jnp.bfloat16)
            dvalue = dot(probs.astype(jnp.bfloat16), cotangents)
            out.append((dot(dscore, queries) * SCALE, dvalue))
            scores.append(dscore)
        keys_t = jnp.concatenate([ktr[head, rr, cc] for rr, cc in places], axis=1)
        dqt[head] += dot(keys_t, jnp.concatenate(scores, axis=0))
        return out

    def give_col(head, rr, cc, grads):
        side = cc // 2
        for kind in range(2):
            col_out[head, rr, side, kind] = grads[kind].astype(jnp.bfloat16)
        slot = 1 - side
        send(
            head, GCOL + 2 * rr + slot, col_out.at[head, rr, side], col_in.at[head, rr, slot],
            col_to[slot], col_sends[slot],
        )

    def second_pass(head):
        dqt[head] = jnp.zeros((HS, 3 * ROWS), jnp.float32)
        for places in (((1, 0), (1, 2)), ((1, 1), (0, 0)), ((0, 2), (0, 1))):
            for (rr, cc), grads in zip(places, key_tiles(head, places)):
                if cc == 1:
                    acc[head, rr, 0], acc[head, rr, 1] = grads
                else:
                    give_col(head, rr, cc, grads)

    def send_row(head):
        for slot in range(2):
            arrive(head, GCOL + 2 + slot, col_in.at[head, 1, slot], col_gets[slot])
        for kind in range(2):
            summed = (
                acc[head, 1, kind]
                + col_in[head, 1, 0, kind].astype(jnp.float32)
                + col_in[head, 1, 1, kind].astype(jnp.float32)
            )
            row_out[head, kind] = summed.astype(jnp.bfloat16)
        send(head, GROW, row_out.at[head], row_in.at[head], partner)

    def send_queries(head):
        for j in range(2):
            dq_out[head, j] = (dqt[head, :, pl.ds(j * ROWS, ROWS)] * SCALE).T.astype(jnp.bfloat16)
        to_owners(head, GQ, dq_out, dq_in.at[head, my_side])

    def finish(head):
        lanes = pl.ds(head * HS, HS)
        for slot in range(2):
            arrive(head, GCOL + slot, col_in.at[head, 0, slot], col_gets[slot])
        arrive(head, GROW, row_in.at[head])
        sums = []
        for kind in range(2):
            sums.append(
                acc[head, 0, kind]
                + col_in[head, 0, 0, kind].astype(jnp.float32)
                + col_in[head, 0, 1, kind].astype(jnp.float32)
                + row_in[head, kind].astype(jnp.float32)
            )
        dk_sum[0, :, lanes] = sums[0]
        dv_sum[0, :, lanes] = sums[1].astype(jnp.bfloat16)
        for slot in range(2):
            arrive(head, GQ + slot, dq_in.at[head, slot], has_site[slot])
        dq_sum[0, :, lanes] = (
            (dqt[head, :, pl.ds(OWN * ROWS, ROWS)] * SCALE).T
            + dq_in[head, 0].astype(jnp.float32)
            + dq_in[head, 1].astype(jnp.float32)
        )

    start_a2a(0)
    gather_first(0)
    start_a2a(1)
    cotangents(0)
    forward_row(0)
    gather_first(1)
    cotangents(1)
    end_cols(0)
    first_pass(0, (OWN,))
    send_own_part(0)
    end_frames(0)
    first_pass(0, (0, 1))
    send_parts(0)
    forward_row(1)
    end_cols(1)
    first_pass(1, (OWN,))
    send_own_part(1)
    end_frames(1)
    first_pass(1, (0, 1))
    send_parts(1)
    totals(0)
    second_pass(0)
    send_queries(0)
    send_row(0)
    totals(1)
    second_pass(1)
    send_queries(1)
    send_row(1)
    finish(0)
    finish(1)
    for cond, wait in started:
        under(cond, wait)


def pull_kernel(q_ref, k_ref, dq_ref, dk_ref, dv_ref, gain_q, gain_k, gq_out, gk_out, gv_out):
    for head in range(2):
        lanes = pl.ds(head * HS, HS)
        for x_ref, d_ref, gain, out in (
            (q_ref, dq_ref, gain_q, gq_out),
            (k_ref, dk_ref, gain_k, gk_out),
        ):
            x = x_ref[0, :, lanes].astype(jnp.float32)
            out[0, :, lanes] = pullback(x, gain[...], d_ref[0, :, lanes]).astype(jnp.bfloat16)
    gv_out[...] = dv_ref[...]


def shards(query, key, value, grad_out, gain_q, gain_k, window):
    half = jax.ShapeDtypeStruct(query.shape, jnp.bfloat16)
    wide = jax.ShapeDtypeStruct(query.shape, jnp.float32)
    vmem = pl.BlockSpec(memory_space=pltpu.VMEM)
    anywhere = pl.BlockSpec(memory_space=pl.ANY)
    low, full = jnp.bfloat16, jnp.float32
    gain_q, gain_k = gain_q.reshape(1, HS), gain_k.reshape(1, HS)
    dquery, dkey, dvalue = pl.pallas_call(
        kernel,
        out_shape=(wide, wide, half),
        in_specs=[pl.BlockSpec(memory_space=pltpu.SMEM)] + [anywhere] * 4 + [vmem] * 2,
        out_specs=(vmem, vmem, vmem),
        scratch_shapes=[
            pltpu.VMEM(query.shape, low),
            pltpu.VMEM(query.shape, low),
            pltpu.VMEM(query.shape, low),
            pltpu.VMEM((2, 2, 3, 2, ROWS, HS), low),
            pltpu.VMEM((2, 2, 3, ROWS, HS), low),
            pltpu.VMEM((2, 2, HS, 3 * ROWS), low),
            pltpu.VMEM((2, 2, 3, HS, ROWS), low),
            pltpu.VMEM((2, 2, 2, ROWS, HS), full),
            pltpu.VMEM((2, HS, 3 * ROWS), full),
            pltpu.VMEM((2, 3, 8, ROWS), full),
            pltpu.VMEM((2, 2, 8, ROWS), full),
            pltpu.VMEM((2, 2, 8, ROWS), full),
            pltpu.VMEM((2, 2, 8, ROWS), full),
            pltpu.VMEM((2, 8, 3 * ROWS), full),
            pltpu.VMEM((2, 2, 2, 2, ROWS, HS), low),
            pltpu.VMEM((2, 2, 2, 2, ROWS, HS), low),
            pltpu.VMEM((2, 2, ROWS, HS), low),
            pltpu.VMEM((2, 2, ROWS, HS), low),
            pltpu.VMEM((2, 2, ROWS, HS), low),
            pltpu.VMEM((2, 2, ROWS, HS), low),
            pltpu.VMEM((2, 2, 3, ROWS, 3 * ROWS), low),
            pltpu.VMEM((2, 2, 3, ROWS, 3 * ROWS), full),
            pltpu.SemaphoreType.DMA((2, COPIES)),
            pltpu.SemaphoreType.DMA((2, COPIES)),
            pltpu.SemaphoreType.DMA((5,)),
        ],
        compiler_params=pltpu.CompilerParams(
            collective_id=0, has_side_effects=True, vmem_limit_bytes=60 * 1024 * 1024
        ),
    )(window, query, key, value, grad_out, gain_q, gain_k)
    return pl.pallas_call(
        pull_kernel,
        out_shape=(half, half, half),
        in_specs=[vmem] * 7,
        out_specs=(vmem, vmem, vmem),
    )(query, key, dquery, dkey, dvalue, gain_q, gain_k)


def solution(mesh):
    placed = (
        P("tile", None, "head"),
        P("tile", None, "head"),
        P("tile", None, "head"),
        P("tile", "head", None),
        P(),
        P(),
        P("head", None),
    )
    return jax.shard_map(
        shards,
        mesh=mesh,
        in_specs=placed,
        out_specs=(P("tile", None, "head"), P("tile", None, "head"), P("tile", None, "head")),
        check_vma=False,
    )
```

```python
import math

import jax
import jax.numpy as jnp
from jax import lax
from jax.experimental import pallas as pl
from jax.experimental.pallas import tpu as pltpu
from jax.sharding import PartitionSpec as P

MESH = pl.DeviceIdType.MESH
HS = 128
TF, TR, TC = 4, 2, 4
ROWS = 384
PIECE = 48
GROUP = 8
PLANE = TR * TC
SCALE = 1.0 / math.sqrt(HS)
EXP_SCALE = SCALE * math.log2(math.e)
EPS = 1e-6

A2A = 0
KVROW = 8
KVCOL = 9
QF = 13
DOF = 15
PART = 17
OWNPART = 19
GCOL = 21
GROW = 25
GQ = 26
OPPOSITE = 28
COPIES = 29

OWN = 2


def dot(a, b):
    return jnp.dot(a, b, preferred_element_type=jnp.float32)


def fold8(x):
    return jnp.sum(x.reshape(x.shape[0] // 8, 8, x.shape[1]), axis=0)


def inv_rms(x):
    return lax.rsqrt(jnp.mean(x * x, axis=-1, keepdims=True) + EPS)


def pullback(x, gain, cotangent):
    rs = inv_rms(x)
    scaled = cotangent * gain
    along = jnp.mean(scaled * x, axis=-1, keepdims=True)
    return rs * scaled - x * (rs * rs * rs * along)


def kernel(
    window, q_hbm, k_hbm, v_hbm, g_ref, gain_q, gain_k,
    dq_sum, dk_sum, dv_sum,
    q_ref, k_ref, v_ref,
    kv, qd, qdt, ktr, acc, dqt, part, part_in, own_in, opp_in, total,
    col_out, col_in, row_out, row_in, dq_out, dq_in, unnorm_kept, dprobs_kept,
    ssem, rsem, lsem,
):
    me = lax.axis_index("head")
    tile = lax.axis_index("tile")
    frame = tile // PLANE
    row = tile // TC % TR
    col = tile % TC
    has_prev, has_next = frame > 0, frame < TF - 1
    has_left, has_right = col > 0, col < TC - 1
    partner = tile + TC * (1 - 2 * row)

    has_remote = jnp.where(row == 0, frame, TF - 1 - frame) > 0
    site = (tile - TC * (1 + row), tile + TC * (2 - row))
    has_site = (has_prev, has_next)
    owner = tuple(tile + TC * (3 * row - 2 + j) for j in range(2))
    my_side = 1 - row
    opposite = tile + 3 * TC * (2 * row - 1)
    has_opposite = jnp.where(row == 0, frame, TF - 1 - frame) > 1

    col_to = (tile + 1, tile - 1)
    col_sends = (has_right, has_left)
    col_gets = (has_left, has_right)

    started = []

    def remote(head, index, src, dst, axis, device, got=None):
        return pltpu.make_async_remote_copy(
            src_ref=src,
            dst_ref=dst,
            send_sem=ssem.at[head, index],
            recv_sem=rsem.at[head, index if got is None else got],
            device_id={axis: device},
            device_id_type=MESH,
        )

    def under(cond, fn):
        if cond is None:
            fn()
        else:
            pl.when(cond)(fn)

    def send(head, index, src, dst, device, cond=None, got=None):
        def copy():
            return remote(head, index, src, dst, "tile", device, got)

        under(cond, lambda: copy().start())
        started.append((cond, lambda: copy().wait_send()))

    def arrive(head, index, dst, cond=None):
        under(cond, lambda: remote(head, index, dst, dst, "tile", partner).wait_recv())

    barrier = pltpu.get_barrier_semaphore()

    def greet(axis, device):
        pl.semaphore_signal(barrier, inc=1, device_id={axis: device}, device_id_type=MESH)

    for step in range(1, GROUP):
        greet("head", lax.rem(me + step, GROUP))
    near = (
        (tile - TC, tile >= TC),
        (tile + TC, tile < TF * PLANE - TC),
        (tile - 2 * TC, has_prev),
        (tile + 2 * TC, has_next),
        (opposite, has_opposite),
        (tile - 1, has_left),
        (tile + 1, has_right),
    )
    for device, cond in near:
        under(cond, lambda device=device: greet("tile", device))

    loads = [
        pltpu.make_async_copy(src, dst, lsem.at[2 + at])
        for at, (src, dst) in enumerate(((k_hbm, k_ref), (v_hbm, v_ref), (q_hbm, q_ref)))
    ]
    for load in loads:
        load.start()
    for load in loads:
        load.wait()

    for head in range(2):
        lanes = pl.ds(head * HS, HS)
        x = k_ref[0, :, lanes].astype(jnp.float32)
        kv[head, 0, 1, 0] = (x * inv_rms(x) * gain_k[...]).astype(jnp.bfloat16)
        kv[head, 0, 1, 1] = v_ref[0, :, lanes]
        x = q_ref[0, :, lanes].astype(jnp.float32)
        qd[head, 0, OWN] = (x * inv_rms(x) * gain_q[...]).astype(jnp.bfloat16)

    def clear(ref):
        ref[...] = jnp.zeros(ref.shape, ref.dtype)

    def no_remote():
        for head in range(2):
            clear(total.at[head])
            for kind in range(2):
                clear(qd.at[head, kind, pl.ds(0, 2)])

    pl.when(jnp.logical_not(has_remote))(no_remote)

    def no_opposite():
        for head in range(2):
            clear(opp_in.at[head])

    pl.when(jnp.logical_not(has_opposite))(no_opposite)

    for slot in range(2):
        def no_site(slot=slot):
            for head in range(2):
                clear(part_in.at[head, slot])
                clear(dq_in.at[head, slot])

        def no_col(slot=slot):
            for head in range(2):
                for rr in range(2):
                    clear(kv.at[head, rr, 2 * slot])
                    clear(col_in.at[head, rr, slot])

        pl.when(jnp.logical_not(has_site[slot]))(no_site)
        pl.when(jnp.logical_not(col_gets[slot]))(no_col)

    greeted = GROUP - 1
    for _, cond in near:
        greeted = greeted + jnp.where(cond, 1, 0)
    pl.semaphore_wait(barrier, greeted)

    def a2a(head, step):
        to = lax.rem(me + step, GROUP)
        src = g_ref.at[0, :, pl.ds(pl.multiple_of(to * (2 * HS) + head * HS, HS), HS)]
        dst = qd.at[head, 1, OWN, pl.ds(pl.multiple_of(me * PIECE, 16), PIECE), :]
        return remote(head, A2A + step, src, dst, "head", to)

    def own_piece(head):
        src = g_ref.at[0, :, pl.ds(pl.multiple_of(me * (2 * HS) + head * HS, HS), HS)]
        dst = qd.at[head, 1, OWN, pl.ds(pl.multiple_of(me * PIECE, 16), PIECE), :]
        return pltpu.make_async_copy(src, dst, lsem.at[head])

    def start_a2a(head):
        for step in range(1, GROUP):
            a2a(head, step).start()
            started.append((None, lambda step=step: a2a(head, step).wait_send()))
        own_piece(head).start()

    def end_a2a(head):
        for step in range(1, GROUP):
            come = lax.rem(me + GROUP - step, GROUP)
            dst = qd.at[head, 1, OWN, pl.ds(pl.multiple_of(come * PIECE, 16), PIECE), :]
            remote(head, A2A + step, dst, dst, "head", come).wait_recv()
        own_piece(head).wait()

    def kv_row(head):
        send(head, KVROW, kv.at[head, 0, 1], kv.at[head, 1, 1], partner)

    def kv_cols(head, rr):
        for slot in range(2):
            send(
                head, KVCOL + 2 * rr + slot, kv.at[head, rr, 1], kv.at[head, rr, 2 * slot],
                col_to[slot], col_sends[slot],
            )

    def to_sites(head, base, src, dst):
        for side in range(2):
            send(head, base + side, src, dst, site[side], has_site[side], base + row)

    def to_owners(head, base, srcs, dst):
        for j in range(2):
            send(head, base + j, srcs.at[head, j], dst, owner[j], has_remote, base + my_side)

    def frames(head, base, kind):
        to_sites(head, base, qd.at[head, kind, OWN], qd.at[head, kind, row])

    def gather_first(head):
        kv_row(head)
        kv_cols(head, 0)
        frames(head, QF, 0)

    def cotangents(head):
        end_a2a(head)
        frames(head, DOF, 1)

    def forward_row(head):
        arrive(head, KVROW, kv.at[head, 1, 1])
        kv_cols(head, 1)

    def end_cols(head):
        for slot in range(2):
            for rr in range(2):
                arrive(head, KVCOL + 2 * rr + slot, kv.at[head, rr, 2 * slot], col_gets[slot])

    def end_frames(head):
        for j in range(2):
            arrive(head, QF + j, qd.at[head, 0, j], has_remote)
            arrive(head, DOF + j, qd.at[head, 1, j], has_remote)

    def one_if(cond):
        return jnp.where(cond, 1, 0)

    def query_mask(head, ff, rr):
        key_row = jnp.where(rr == 0, row, 1 - row)
        offset = key_row - (0, 1, row)[ff]
        rows = jnp.where(offset == 0, 1, jnp.where(offset > 0, window[head, 3], -window[head, 2]))
        if ff == OWN:
            return rows
        frames = jnp.where(row == 0, window[head, 1], -window[head, 0])
        return rows * frames * one_if(has_remote)

    def col_mask(head, cc):
        left = -window[head, 4] * one_if(has_left)
        right = window[head, 5] * one_if(has_right)
        return jnp.where(cc == 0, left, jnp.where(cc == 2, right, 1))

    def live(head, rr, cc, ff):
        return jnp.where(col_mask(head, cc) * query_mask(head, ff, rr) == 1, 1.0, 0.0)

    def first_pass(head, ffs):
        lanes = pl.ds(ffs[0] * ROWS, len(ffs) * ROWS)
        for ff in ffs:
            for kind in range(2):
                qdt[head, kind, :, pl.ds(ff * ROWS, ROWS)] = qd[head, kind, ff].T

        def body(i, carry):
            rr, cc = i // 3, i % 3
            keys, values = kv[head, rr, cc, 0], kv[head, rr, cc, 1]
            if OWN in ffs:
                ktr[head, rr, cc] = keys.T
            unnorm = jnp.exp2(dot(keys, qdt[head, 0, :, lanes]) * EXP_SCALE)
            dprobs = dot(values, qdt[head, 1, :, lanes])
            unnorm_kept[head, rr, cc, :, lanes] = unnorm.astype(jnp.bfloat16)
            dprobs_kept[head, rr, cc, :, lanes] = dprobs
            sums = (fold8(unnorm), fold8(unnorm * dprobs))
            out = []
            for at, ff in enumerate(ffs):
                here = live(head, rr, cc, ff)
                for kind in range(2):
                    mine = sums[kind][:, at * ROWS : (at + 1) * ROWS]
                    out.append(carry[2 * at + kind] + mine * here)
            return tuple(out)

        zero = jnp.zeros((8, ROWS), jnp.float32)
        sums = lax.fori_loop(0, 6, body, (zero,) * (2 * len(ffs)), unroll=6)
        for at, ff in enumerate(ffs):
            for kind in range(2):
                part[head, ff, kind : kind + 1] = jnp.sum(
                    sums[2 * at + kind], axis=0, keepdims=True
                )

    def send_own_part(head):
        to_sites(head, OWNPART, part.at[head, OWN], own_in.at[head, row])

    def send_parts(head):
        to_owners(head, PART, part, part_in.at[head, my_side])
        send(
            head, OPPOSITE, part.at[head, pl.ds(0, 2)], opp_in.at[head], opposite, has_opposite
        )

    def totals(head):
        def put(ff, terms):
            both = part[head, ff] + terms[0] + terms[1]
            lanes = pl.ds(ff * ROWS, ROWS)
            total[head, 0:1, lanes] = 1.0 / both[0:1]
            total[head, 1:2, lanes] = both[1:2] / both[0:1]

        for slot in range(2):
            arrive(head, PART + slot, part_in.at[head, slot], has_site[slot])
        put(OWN, (part_in[head, 0], part_in[head, 1]))
        for j in range(2):
            arrive(head, OWNPART + j, own_in.at[head, j], has_remote)
        arrive(head, OPPOSITE, opp_in.at[head], has_opposite)

        def put_remote():
            for j in range(2):
                put(j, (own_in[head, j], opp_in[head, j]))

        pl.when(has_remote)(put_remote)

    def key_tiles(head, places):
        queries = qd[head, 0].reshape(3 * ROWS, HS)
        cotangents = qd[head, 1].reshape(3 * ROWS, HS)
        centre = total[head, 1:2]
        out, scores = [], []
        for rr, cc in places:
            alive = jnp.concatenate(
                [jnp.full((1, ROWS), live(head, rr, cc, ff), jnp.float32) for ff in range(3)],
                axis=1,
            )
            share = total[head, 0:1] * alive
            probs = unnorm_kept[head, rr, cc].astype(jnp.float32) * share
            dscore = (probs * (dprobs_kept[head, rr, cc] - centre)).astype(jnp.bfloat16)
            dvalue = dot(probs.astype(jnp.bfloat16), cotangents)
            out.append((dot(dscore, queries) * SCALE, dvalue))
            scores.append(dscore)
        keys_t = jnp.concatenate([ktr[head, rr, cc] for rr, cc in places], axis=1)
        dqt[head] += dot(keys_t, jnp.concatenate(scores, axis=0))
        return out

    def give_col(head, rr, cc, grads):
        side = cc // 2
        for kind in range(2):
            col_out[head, rr, side, kind] = grads[kind].astype(jnp.bfloat16)
        slot = 1 - side
        send(
            head, GCOL + 2 * rr + slot, col_out.at[head, rr, side], col_in.at[head, rr, slot],
            col_to[slot], col_sends[slot],
        )

    def second_pass(head):
        dqt[head] = jnp.zeros((HS, 3 * ROWS), jnp.float32)
        for places in (((1, 0), (1, 2)), ((1, 1), (0, 0)), ((0, 2), (0, 1))):
            for (rr, cc), grads in zip(places, key_tiles(head, places)):
                if cc == 1:
                    acc[head, rr, 0], acc[head, rr, 1] = grads
                else:
                    give_col(head, rr, cc, grads)

    def send_row(head):
        for slot in range(2):
            arrive(head, GCOL + 2 + slot, col_in.at[head, 1, slot], col_gets[slot])
        for kind in range(2):
            summed = (
                acc[head, 1, kind]
                + col_in[head, 1, 0, kind].astype(jnp.float32)
                + col_in[head, 1, 1, kind].astype(jnp.float32)
            )
            row_out[head, kind] = summed.astype(jnp.bfloat16)
        send(head, GROW, row_out.at[head], row_in.at[head], partner)

    def send_queries(head):
        for j in range(2):
            dq_out[head, j] = (dqt[head, :, pl.ds(j * ROWS, ROWS)] * SCALE).T.astype(jnp.bfloat16)
        to_owners(head, GQ, dq_out, dq_in.at[head, my_side])

    def finish(head):
        lanes = pl.ds(head * HS, HS)
        for slot in range(2):
            arrive(head, GCOL + slot, col_in.at[head, 0, slot], col_gets[slot])
        arrive(head, GROW, row_in.at[head])
        sums = []
        for kind in range(2):
            sums.append(
                acc[head, 0, kind]
                + col_in[head, 0, 0, kind].astype(jnp.float32)
                + col_in[head, 0, 1, kind].astype(jnp.float32)
                + row_in[head, kind].astype(jnp.float32)
            )
        dk_sum[0, :, lanes] = sums[0]
        dv_sum[0, :, lanes] = sums[1].astype(jnp.bfloat16)
        for slot in range(2):
            arrive(head, GQ + slot, dq_in.at[head, slot], has_site[slot])
        dq_sum[0, :, lanes] = (
            (dqt[head, :, pl.ds(OWN * ROWS, ROWS)] * SCALE).T
            + dq_in[head, 0].astype(jnp.float32)
            + dq_in[head, 1].astype(jnp.float32)
        )

    start_a2a(0)
    gather_first(0)
    start_a2a(1)
    frames(1, QF, 0)
    cotangents(0)
    forward_row(0)
    kv_row(1)
    kv_cols(1, 0)
    cotangents(1)
    end_cols(0)
    first_pass(0, (OWN,))
    send_own_part(0)
    end_frames(0)
    first_pass(0, (0, 1))
    send_parts(0)
    forward_row(1)
    end_cols(1)
    first_pass(1, (OWN,))
    send_own_part(1)
    end_frames(1)
    first_pass(1, (0, 1))
    send_parts(1)
    totals(0)
    second_pass(0)
    send_queries(0)
    send_row(0)
    totals(1)
    second_pass(1)
    send_queries(1)
    send_row(1)
    finish(0)
    finish(1)
    for cond, wait in started:
        under(cond, wait)


def pull_kernel(q_ref, k_ref, dq_ref, dk_ref, dv_ref, gain_q, gain_k, gq_out, gk_out, gv_out):
    for head in range(2):
        lanes = pl.ds(head * HS, HS)
        for x_ref, d_ref, gain, out in (
            (q_ref, dq_ref, gain_q, gq_out),
            (k_ref, dk_ref, gain_k, gk_out),
        ):
            x = x_ref[0, :, lanes].astype(jnp.float32)
            out[0, :, lanes] = pullback(x, gain[...], d_ref[0, :, lanes]).astype(jnp.bfloat16)
    gv_out[...] = dv_ref[...]


def shards(query, key, value, grad_out, gain_q, gain_k, window):
    half = jax.ShapeDtypeStruct(query.shape, jnp.bfloat16)
    wide = jax.ShapeDtypeStruct(query.shape, jnp.float32)
    vmem = pl.BlockSpec(memory_space=pltpu.VMEM)
    anywhere = pl.BlockSpec(memory_space=pl.ANY)
    low, full = jnp.bfloat16, jnp.float32
    gain_q, gain_k = gain_q.reshape(1, HS), gain_k.reshape(1, HS)
    dquery, dkey, dvalue = pl.pallas_call(
        kernel,
        out_shape=(wide, wide, half),
        in_specs=[pl.BlockSpec(memory_space=pltpu.SMEM)] + [anywhere] * 4 + [vmem] * 2,
        out_specs=(vmem, vmem, vmem),
        scratch_shapes=[
            pltpu.VMEM(query.shape, low),
            pltpu.VMEM(query.shape, low),
            pltpu.VMEM(query.shape, low),
            pltpu.VMEM((2, 2, 3, 2, ROWS, HS), low),
            pltpu.VMEM((2, 2, 3, ROWS, HS), low),
            pltpu.VMEM((2, 2, HS, 3 * ROWS), low),
            pltpu.VMEM((2, 2, 3, HS, ROWS), low),
            pltpu.VMEM((2, 2, 2, ROWS, HS), full),
            pltpu.VMEM((2, HS, 3 * ROWS), full),
            pltpu.VMEM((2, 3, 2, ROWS), full),
            pltpu.VMEM((2, 2, 2, ROWS), full),
            pltpu.VMEM((2, 2, 2, ROWS), full),
            pltpu.VMEM((2, 2, 2, ROWS), full),
            pltpu.VMEM((2, 8, 3 * ROWS), full),
            pltpu.VMEM((2, 2, 2, 2, ROWS, HS), low),
            pltpu.VMEM((2, 2, 2, 2, ROWS, HS), low),
            pltpu.VMEM((2, 2, ROWS, HS), low),
            pltpu.VMEM((2, 2, ROWS, HS), low),
            pltpu.VMEM((2, 2, ROWS, HS), low),
            pltpu.VMEM((2, 2, ROWS, HS), low),
            pltpu.VMEM((2, 2, 3, ROWS, 3 * ROWS), low),
            pltpu.VMEM((2, 2, 3, ROWS, 3 * ROWS), full),
            pltpu.SemaphoreType.DMA((2, COPIES)),
            pltpu.SemaphoreType.DMA((2, COPIES)),
            pltpu.SemaphoreType.DMA((5,)),
        ],
        compiler_params=pltpu.CompilerParams(
            collective_id=0, has_side_effects=True, vmem_limit_bytes=60 * 1024 * 1024
        ),
    )(window, query, key, value, grad_out, gain_q, gain_k)
    return pl.pallas_call(
        pull_kernel,
        out_shape=(half, half, half),
        in_specs=[vmem] * 7,
        out_specs=(vmem, vmem, vmem),
    )(query, key, dquery, dkey, dvalue, gain_q, gain_k)


def solution(mesh):
    placed = (
        P("tile", None, "head"),
        P("tile", None, "head"),
        P("tile", None, "head"),
        P("tile", "head", None),
        P(),
        P(),
        P("head", None),
    )
    return jax.shard_map(
        shards,
        mesh=mesh,
        in_specs=placed,
        out_specs=(P("tile", None, "head"), P("tile", None, "head"), P("tile", None, "head")),
        check_vma=False,
    )
```

```python
import math

import jax
import jax.numpy as jnp
from jax import lax
from jax.experimental import pallas as pl
from jax.experimental.pallas import tpu as pltpu
from jax.sharding import PartitionSpec as P

MESH = pl.DeviceIdType.MESH
HS = 128
TF, TR, TC = 4, 2, 4
ROWS = 384
PIECE = 48
GROUP = 8
PLANE = TR * TC
SCALE = 1.0 / math.sqrt(HS)
EXP_SCALE = SCALE * math.log2(math.e)
EPS = 1e-6

A2A = 0
KVROW = 8
KVCOL = 9
QF = 13
DOF = 15
PART = 17
OWNPART = 19
GCOL = 21
GROW = 25
GQ = 26
OPPOSITE = 28
COPIES = 29

OWN = 2


def dot(a, b):
    return jnp.dot(a, b, preferred_element_type=jnp.float32)


def fold8(x):
    return jnp.sum(x.reshape(x.shape[0] // 8, 8, x.shape[1]), axis=0)


def inv_rms(x):
    return lax.rsqrt(jnp.mean(x * x, axis=-1, keepdims=True) + EPS)


def pullback(x, gain, cotangent):
    rs = inv_rms(x)
    scaled = cotangent * gain
    along = jnp.mean(scaled * x, axis=-1, keepdims=True)
    return rs * scaled - x * (rs * rs * rs * along)


def kernel(
    window, q_hbm, k_hbm, v_hbm, g_ref, gain_q, gain_k,
    dq_sum, dk_sum, dv_sum,
    q_ref, k_ref, v_ref,
    kv, qd, qdt, ktr, acc, dqt, part, part_in, own_in, opp_in, total,
    col_out, col_in, row_out, row_in, dq_out, dq_in, unnorm_kept, dprobs_kept,
    ssem, rsem, lsem,
):
    me = lax.axis_index("head")
    tile = lax.axis_index("tile")
    frame = tile // PLANE
    row = tile // TC % TR
    col = tile % TC
    has_prev, has_next = frame > 0, frame < TF - 1
    has_left, has_right = col > 0, col < TC - 1
    partner = tile + TC * (1 - 2 * row)

    has_remote = jnp.where(row == 0, frame, TF - 1 - frame) > 0
    site = (tile - TC * (1 + row), tile + TC * (2 - row))
    has_site = (has_prev, has_next)
    owner = tuple(tile + TC * (3 * row - 2 + j) for j in range(2))
    my_side = 1 - row
    opposite = tile + 3 * TC * (2 * row - 1)
    has_opposite = jnp.where(row == 0, frame, TF - 1 - frame) > 1

    col_to = (tile + 1, tile - 1)
    col_sends = (has_right, has_left)
    col_gets = (has_left, has_right)

    started = []

    def remote(head, index, src, dst, axis, device, got=None):
        return pltpu.make_async_remote_copy(
            src_ref=src,
            dst_ref=dst,
            send_sem=ssem.at[head, index],
            recv_sem=rsem.at[head, index if got is None else got],
            device_id={axis: device},
            device_id_type=MESH,
        )

    def under(cond, fn):
        if cond is None:
            fn()
        else:
            pl.when(cond)(fn)

    def send(head, index, src, dst, device, cond=None, got=None):
        def copy():
            return remote(head, index, src, dst, "tile", device, got)

        under(cond, lambda: copy().start())
        started.append((cond, lambda: copy().wait_send()))

    def arrive(head, index, dst, cond=None):
        under(cond, lambda: remote(head, index, dst, dst, "tile", partner).wait_recv())

    barrier = pltpu.get_barrier_semaphore()

    def greet(axis, device):
        pl.semaphore_signal(barrier, inc=1, device_id={axis: device}, device_id_type=MESH)

    for step in range(1, GROUP):
        greet("head", lax.rem(me + step, GROUP))
    near = (
        (tile - TC, tile >= TC),
        (tile + TC, tile < TF * PLANE - TC),
        (tile - 2 * TC, has_prev),
        (tile + 2 * TC, has_next),
        (opposite, has_opposite),
        (tile - 1, has_left),
        (tile + 1, has_right),
    )
    for device, cond in near:
        under(cond, lambda device=device: greet("tile", device))

    loads = [
        pltpu.make_async_copy(src, dst, lsem.at[2 + at])
        for at, (src, dst) in enumerate(((k_hbm, k_ref), (v_hbm, v_ref), (q_hbm, q_ref)))
    ]
    for load in loads:
        load.start()
    for load in loads:
        load.wait()

    for head in range(2):
        lanes = pl.ds(head * HS, HS)
        x = k_ref[0, :, lanes].astype(jnp.float32)
        kv[head, 0, 1, 0] = (x * inv_rms(x) * gain_k[...]).astype(jnp.bfloat16)
        kv[head, 0, 1, 1] = v_ref[0, :, lanes]
        x = q_ref[0, :, lanes].astype(jnp.float32)
        qd[head, 0, OWN] = (x * inv_rms(x) * gain_q[...]).astype(jnp.bfloat16)

    def clear(ref):
        ref[...] = jnp.zeros(ref.shape, ref.dtype)

    def no_remote():
        for head in range(2):
            clear(total.at[head])
            for kind in range(2):
                clear(qd.at[head, kind, pl.ds(0, 2)])

    pl.when(jnp.logical_not(has_remote))(no_remote)

    def no_opposite():
        for head in range(2):
            clear(opp_in.at[head])

    pl.when(jnp.logical_not(has_opposite))(no_opposite)

    for slot in range(2):
        def no_site(slot=slot):
            for head in range(2):
                clear(part_in.at[head, slot])
                clear(dq_in.at[head, slot])

        def no_col(slot=slot):
            for head in range(2):
                for rr in range(2):
                    clear(kv.at[head, rr, 2 * slot])
                    clear(col_in.at[head, rr, slot])

        pl.when(jnp.logical_not(has_site[slot]))(no_site)
        pl.when(jnp.logical_not(col_gets[slot]))(no_col)

    greeted = GROUP - 1
    for _, cond in near:
        greeted = greeted + jnp.where(cond, 1, 0)
    pl.semaphore_wait(barrier, greeted)

    def a2a(head, step):
        to = lax.rem(me + step, GROUP)
        src = g_ref.at[0, :, pl.ds(pl.multiple_of(to * (2 * HS) + head * HS, HS), HS)]
        dst = qd.at[head, 1, OWN, pl.ds(pl.multiple_of(me * PIECE, 16), PIECE), :]
        return remote(head, A2A + step, src, dst, "head", to)

    def own_piece(head):
        src = g_ref.at[0, :, pl.ds(pl.multiple_of(me * (2 * HS) + head * HS, HS), HS)]
        dst = qd.at[head, 1, OWN, pl.ds(pl.multiple_of(me * PIECE, 16), PIECE), :]
        return pltpu.make_async_copy(src, dst, lsem.at[head])

    def start_a2a(head):
        for step in range(1, GROUP):
            a2a(head, step).start()
            started.append((None, lambda step=step: a2a(head, step).wait_send()))
        own_piece(head).start()

    def end_a2a(head):
        for step in range(1, GROUP):
            come = lax.rem(me + GROUP - step, GROUP)
            dst = qd.at[head, 1, OWN, pl.ds(pl.multiple_of(come * PIECE, 16), PIECE), :]
            remote(head, A2A + step, dst, dst, "head", come).wait_recv()
        own_piece(head).wait()

    def kv_row(head):
        send(head, KVROW, kv.at[head, 0, 1], kv.at[head, 1, 1], partner)

    def kv_cols(head, rr):
        for slot in range(2):
            send(
                head, KVCOL + 2 * rr + slot, kv.at[head, rr, 1], kv.at[head, rr, 2 * slot],
                col_to[slot], col_sends[slot],
            )

    def to_sites(head, base, src, dst):
        for side in range(2):
            send(head, base + side, src, dst, site[side], has_site[side], base + row)

    def to_owners(head, base, srcs, dst):
        for j in range(2):
            send(head, base + j, srcs.at[head, j], dst, owner[j], has_remote, base + my_side)

    def frames(head, base, kind):
        to_sites(head, base, qd.at[head, kind, OWN], qd.at[head, kind, row])

    def gather_first(head):
        kv_row(head)
        frames(head, QF, 0)
        kv_cols(head, 0)

    def cotangents(head):
        end_a2a(head)
        frames(head, DOF, 1)

    def forward_row(head):
        arrive(head, KVROW, kv.at[head, 1, 1])
        kv_cols(head, 1)

    def end_cols(head):
        for slot in range(2):
            for rr in range(2):
                arrive(head, KVCOL + 2 * rr + slot, kv.at[head, rr, 2 * slot], col_gets[slot])

    def end_frames(head):
        for j in range(2):
            arrive(head, QF + j, qd.at[head, 0, j], has_remote)
            arrive(head, DOF + j, qd.at[head, 1, j], has_remote)

    def one_if(cond):
        return jnp.where(cond, 1, 0)

    def query_mask(head, ff, rr):
        key_row = jnp.where(rr == 0, row, 1 - row)
        offset = key_row - (0, 1, row)[ff]
        rows = jnp.where(offset == 0, 1, jnp.where(offset > 0, window[head, 3], -window[head, 2]))
        if ff == OWN:
            return rows
        frames = jnp.where(row == 0, window[head, 1], -window[head, 0])
        return rows * frames * one_if(has_remote)

    def col_mask(head, cc):
        left = -window[head, 4] * one_if(has_left)
        right = window[head, 5] * one_if(has_right)
        return jnp.where(cc == 0, left, jnp.where(cc == 2, right, 1))

    def live(head, rr, cc, ff):
        return jnp.where(col_mask(head, cc) * query_mask(head, ff, rr) == 1, 1.0, 0.0)

    def first_pass(head, ffs):
        lanes = pl.ds(ffs[0] * ROWS, len(ffs) * ROWS)
        for ff in ffs:
            for kind in range(2):
                qdt[head, kind, :, pl.ds(ff * ROWS, ROWS)] = qd[head, kind, ff].T

        def body(i, carry):
            rr, cc = i // 3, i % 3
            keys, values = kv[head, rr, cc, 0], kv[head, rr, cc, 1]
            if OWN in ffs:
                ktr[head, rr, cc] = keys.T
            unnorm = jnp.exp2(dot(keys, qdt[head, 0, :, lanes]) * EXP_SCALE)
            dprobs = dot(values, qdt[head, 1, :, lanes])
            unnorm_kept[head, rr, cc, :, lanes] = unnorm.astype(jnp.bfloat16)
            dprobs_kept[head, rr, cc, :, lanes] = dprobs
            sums = (fold8(unnorm), fold8(unnorm * dprobs))
            out = []
            for at, ff in enumerate(ffs):
                here = live(head, rr, cc, ff)
                for kind in range(2):
                    mine = sums[kind][:, at * ROWS : (at + 1) * ROWS]
                    out.append(carry[2 * at + kind] + mine * here)
            return tuple(out)

        zero = jnp.zeros((8, ROWS), jnp.float32)
        sums = lax.fori_loop(0, 6, body, (zero,) * (2 * len(ffs)), unroll=6)
        for at, ff in enumerate(ffs):
            for kind in range(2):
                part[head, ff, kind : kind + 1] = jnp.sum(
                    sums[2 * at + kind], axis=0, keepdims=True
                )

    def send_own_part(head):
        to_sites(head, OWNPART, part.at[head, OWN], own_in.at[head, row])

    def send_parts(head):
        to_owners(head, PART, part, part_in.at[head, my_side])
        send(
            head, OPPOSITE, part.at[head, pl.ds(0, 2)], opp_in.at[head], opposite, has_opposite
        )

    def totals(head):
        def put(ff, terms):
            both = part[head, ff] + terms[0] + terms[1]
            lanes = pl.ds(ff * ROWS, ROWS)
            total[head, 0:1, lanes] = 1.0 / both[0:1]
            total[head, 1:2, lanes] = both[1:2] / both[0:1]

        for slot in range(2):
            arrive(head, PART + slot, part_in.at[head, slot], has_site[slot])
        put(OWN, (part_in[head, 0], part_in[head, 1]))
        for j in range(2):
            arrive(head, OWNPART + j, own_in.at[head, j], has_remote)
        arrive(head, OPPOSITE, opp_in.at[head], has_opposite)

        def put_remote():
            for j in range(2):
                put(j, (own_in[head, j], opp_in[head, j]))

        pl.when(has_remote)(put_remote)

    def key_tiles(head, places):
        queries = qd[head, 0].reshape(3 * ROWS, HS)
        cotangents = qd[head, 1].reshape(3 * ROWS, HS)
        centre = total[head, 1:2]
        out, scores = [], []
        for rr, cc in places:
            alive = jnp.concatenate(
                [jnp.full((1, ROWS), live(head, rr, cc, ff), jnp.float32) for ff in range(3)],
                axis=1,
            )
            share = total[head, 0:1] * alive
            probs = unnorm_kept[head, rr, cc].astype(jnp.float32) * share
            dscore = (probs * (dprobs_kept[head, rr, cc] - centre)).astype(jnp.bfloat16)
            dvalue = dot(probs.astype(jnp.bfloat16), cotangents)
            out.append((dot(dscore, queries) * SCALE, dvalue))
            scores.append(dscore)
        keys_t = jnp.concatenate([ktr[head, rr, cc] for rr, cc in places], axis=1)
        dqt[head] += dot(keys_t, jnp.concatenate(scores, axis=0))
        return out

    def give_col(head, rr, cc, grads):
        side = cc // 2
        for kind in range(2):
            col_out[head, rr, side, kind] = grads[kind].astype(jnp.bfloat16)
        slot = 1 - side
        send(
            head, GCOL + 2 * rr + slot, col_out.at[head, rr, side], col_in.at[head, rr, slot],
            col_to[slot], col_sends[slot],
        )

    def second_pass(head):
        dqt[head] = jnp.zeros((HS, 3 * ROWS), jnp.float32)
        for places in (((1, 0), (1, 2)), ((1, 1), (0, 0)), ((0, 2), (0, 1))):
            for (rr, cc), grads in zip(places, key_tiles(head, places)):
                if cc == 1:
                    acc[head, rr, 0], acc[head, rr, 1] = grads
                else:
                    give_col(head, rr, cc, grads)

    def send_row(head):
        for slot in range(2):
            arrive(head, GCOL + 2 + slot, col_in.at[head, 1, slot], col_gets[slot])
        for kind in range(2):
            summed = (
                acc[head, 1, kind]
                + col_in[head, 1, 0, kind].astype(jnp.float32)
                + col_in[head, 1, 1, kind].astype(jnp.float32)
            )
            row_out[head, kind] = summed.astype(jnp.bfloat16)
        send(head, GROW, row_out.at[head], row_in.at[head], partner)

    def send_queries(head):
        for j in range(2):
            dq_out[head, j] = (dqt[head, :, pl.ds(j * ROWS, ROWS)] * SCALE).T.astype(jnp.bfloat16)
        to_owners(head, GQ, dq_out, dq_in.at[head, my_side])

    def finish(head):
        lanes = pl.ds(head * HS, HS)
        for slot in range(2):
            arrive(head, GCOL + slot, col_in.at[head, 0, slot], col_gets[slot])
        arrive(head, GROW, row_in.at[head])
        sums = []
        for kind in range(2):
            sums.append(
                acc[head, 0, kind]
                + col_in[head, 0, 0, kind].astype(jnp.float32)
                + col_in[head, 0, 1, kind].astype(jnp.float32)
                + row_in[head, kind].astype(jnp.float32)
            )
        dk_sum[0, :, lanes] = sums[0]
        dv_sum[0, :, lanes] = sums[1].astype(jnp.bfloat16)
        for slot in range(2):
            arrive(head, GQ + slot, dq_in.at[head, slot], has_site[slot])
        dq_sum[0, :, lanes] = (
            (dqt[head, :, pl.ds(OWN * ROWS, ROWS)] * SCALE).T
            + dq_in[head, 0].astype(jnp.float32)
            + dq_in[head, 1].astype(jnp.float32)
        )

    start_a2a(0)
    gather_first(0)
    start_a2a(1)
    frames(1, QF, 0)
    cotangents(0)
    forward_row(0)
    kv_row(1)
    cotangents(1)
    kv_cols(1, 0)
    end_cols(0)
    first_pass(0, (OWN,))
    send_own_part(0)
    end_frames(0)
    first_pass(0, (0, 1))
    send_parts(0)
    forward_row(1)
    end_cols(1)
    first_pass(1, (OWN,))
    send_own_part(1)
    end_frames(1)
    first_pass(1, (0, 1))
    send_parts(1)
    totals(0)
    second_pass(0)
    send_queries(0)
    send_row(0)
    totals(1)
    before = len(started)
    second_pass(1)
    send_queries(1)
    send_row(1)
    for cond, wait in started[:before]:
        under(cond, wait)
    finish(0)
    finish(1)
    for cond, wait in started[before:]:
        under(cond, wait)


def pull_kernel(q_ref, k_ref, dq_ref, dk_ref, dv_ref, gain_q, gain_k, gq_out, gk_out, gv_out):
    for head in range(2):
        lanes = pl.ds(head * HS, HS)
        for x_ref, d_ref, gain, out in (
            (q_ref, dq_ref, gain_q, gq_out),
            (k_ref, dk_ref, gain_k, gk_out),
        ):
            x = x_ref[0, :, lanes].astype(jnp.float32)
            out[0, :, lanes] = pullback(x, gain[...], d_ref[0, :, lanes]).astype(jnp.bfloat16)
    gv_out[...] = dv_ref[...]


def shards(query, key, value, grad_out, gain_q, gain_k, window):
    half = jax.ShapeDtypeStruct(query.shape, jnp.bfloat16)
    wide = jax.ShapeDtypeStruct(query.shape, jnp.float32)
    vmem = pl.BlockSpec(memory_space=pltpu.VMEM)
    anywhere = pl.BlockSpec(memory_space=pl.ANY)
    low, full = jnp.bfloat16, jnp.float32
    gain_q, gain_k = gain_q.reshape(1, HS), gain_k.reshape(1, HS)
    dquery, dkey, dvalue = pl.pallas_call(
        kernel,
        out_shape=(wide, wide, half),
        in_specs=[pl.BlockSpec(memory_space=pltpu.SMEM)] + [anywhere] * 4 + [vmem] * 2,
        out_specs=(vmem, vmem, vmem),
        scratch_shapes=[
            pltpu.VMEM(query.shape, low),
            pltpu.VMEM(query.shape, low),
            pltpu.VMEM(query.shape, low),
            pltpu.VMEM((2, 2, 3, 2, ROWS, HS), low),
            pltpu.VMEM((2, 2, 3, ROWS, HS), low),
            pltpu.VMEM((2, 2, HS, 3 * ROWS), low),
            pltpu.VMEM((2, 2, 3, HS, ROWS), low),
            pltpu.VMEM((2, 2, 2, ROWS, HS), full),
            pltpu.VMEM((2, HS, 3 * ROWS), full),
            pltpu.VMEM((2, 3, 2, ROWS), full),
            pltpu.VMEM((2, 2, 2, ROWS), full),
            pltpu.VMEM((2, 2, 2, ROWS), full),
            pltpu.VMEM((2, 2, 2, ROWS), full),
            pltpu.VMEM((2, 8, 3 * ROWS), full),
            pltpu.VMEM((2, 2, 2, 2, ROWS, HS), low),
            pltpu.VMEM((2, 2, 2, 2, ROWS, HS), low),
            pltpu.VMEM((2, 2, ROWS, HS), low),
            pltpu.VMEM((2, 2, ROWS, HS), low),
            pltpu.VMEM((2, 2, ROWS, HS), low),
            pltpu.VMEM((2, 2, ROWS, HS), low),
            pltpu.VMEM((2, 2, 3, ROWS, 3 * ROWS), low),
            pltpu.VMEM((2, 2, 3, ROWS, 3 * ROWS), full),
            pltpu.SemaphoreType.DMA((2, COPIES)),
            pltpu.SemaphoreType.DMA((2, COPIES)),
            pltpu.SemaphoreType.DMA((5,)),
        ],
        compiler_params=pltpu.CompilerParams(
            collective_id=0, has_side_effects=True, vmem_limit_bytes=60 * 1024 * 1024
        ),
    )(window, query, key, value, grad_out, gain_q, gain_k)
    return pl.pallas_call(
        pull_kernel,
        out_shape=(half, half, half),
        in_specs=[vmem] * 7,
        out_specs=(vmem, vmem, vmem),
    )(query, key, dquery, dkey, dvalue, gain_q, gain_k)


def solution(mesh):
    placed = (
        P("tile", None, "head"),
        P("tile", None, "head"),
        P("tile", None, "head"),
        P("tile", "head", None),
        P(),
        P(),
        P("head", None),
    )
    return jax.shard_map(
        shards,
        mesh=mesh,
        in_specs=placed,
        out_specs=(P("tile", None, "head"), P("tile", None, "head"), P("tile", None, "head")),
        check_vma=False,
    )
```
